32 devices in a mesh: dev: 16 (over z, y, x), head: 2 (over core).
Axes of the slice: x: 2, y: 2, z: 4, core: 2. Of those that a mesh axis runs over, the one named last changes fastest.
Arguments:
- tokens: bfloat16 [60, 512, 768], P(None, ('head', 'dev')), may hold values from -6 to 6
- lengths: int32 [60, 4], replicated, may hold values from 1 to 448, 512 in all within a row
- w_in: bfloat16 [2, 3, 768, 768], P(None, None, None, 'head'), may hold values from -0.21875 to 0.21875
- b_in: bfloat16 [2, 2, 768], P(None, None, 'head'), may hold values from -4 to 4
- w_out: bfloat16 [2, 768, 768], P(None, 'head'), may hold values from -0.625 to 0.625
- w_up: bfloat16 [2, 768, 3072], P(None, None, 'head'), may hold values from -0.21875 to 0.21875
- b_up: bfloat16 [2, 3072], P(None, 'head'), may hold values from -4 to 4
- w_down: bfloat16 [2, 3072, 768], P(None, 'head'), may hold values from -0.109375 to 0.109375
- norm_gain: float32 [2, 2, 768], replicated, may hold values from 0.5 to 1.5
- norm_bias: float32 [2, 4, 768], replicated, may hold values from -4 to 4
- rel_table: float32 [2, 12, 512], P(None, 'head'), may hold values from -6 to 6
- d_pooled: bfloat16 [60, 256, 768], P(None, ('head', 'dev')), may hold values from -6 to 6
- d_skip: bfloat16 [60, 512, 768], P(None, ('head', 'dev')), may hold values from -6 to 6
Outputs:
- pooled_out: bfloat16 [60, 256, 768], P(None, ('head', 'dev'))
- skip_sum: bfloat16 [60, 512, 768], P(None, ('head', 'dev'))
- d_input: bfloat16 [60, 512, 768], P(None, ('head', 'dev'))
- g_w_in: float32 [2, 3, 768, 768], P(None, None, None, 'head')
- g_b_in: float32 [2, 2, 768], P(None, None, 'head')
- g_w_out: float32 [2, 768, 768], P(None, 'head')
- g_w_up: float32 [2, 768, 3072], P(None, None, 'head')
- g_b_up: float32 [2, 3072], P(None, 'head')
- g_w_down: float32 [2, 3072, 768], P(None, 'head')
- g_norm_gain: float32 [2, 2, 768], P(None, None, 'head')
- g_norm_bias: float32 [2, 4, 768], P(None, None, 'head')
- g_rel: float32 [2, 12, 512], P(None, 'head')
The draws below stay inside these ranges and needn't reach their ends.
Inputs may be any that keep to these rules, and one draw needn't show every extreme that they name: Each row's 4 document lengths sum to 512, and every row's longest document has exactly 448 tokens.
All inputs are finite; a program needn't handle non-finite values.
Results may differ from the reference program's by a relative error of at most 0.024.
Values may be sent and summed in bfloat16 or wider, within the bound.
No kernel may reach another device: no remote copies, remote signals or barrier semaphores. Data moves between devices by JAX's collectives and lax.ppermute only.
A program may use at most 384 MiB of HBM per device.

```python
import math
import jax
import jax.numpy as jnp
import numpy as np
from jax import lax

D = 768
HEADS = 12
HEAD_DIM = 64
FF = 3072
SEQ = 512
NDOC = 4
POOLED = 256
ROWS = 60


def steps_of(own_key, dims, cuts, smallest, largest):
    def one(axis_at, blocks):
        draws = jax.random.uniform(jax.random.fold_in(jax.random.fold_in(own_key, 6), axis_at), (blocks,), jnp.float32, smallest / len(cuts), largest / len(cuts))
        return jnp.repeat(jnp.exp(draws), dims[axis_at] // blocks).reshape((-1,) + (1,) * (len(dims) - axis_at - 1))

    level = one(*cuts[0])
    for cut in cuts[1:]:
        level = level * one(*cut)
    return level


def split_up(count, total, reach, skew):
    portions = [(1 << 20) // math.isqrt(standing ** skew) + 1 for standing in range(2, count + 1)]
    surplus, counts = total - reach - (count - 1), [1] * (count - 1)
    while surplus > 0:
        candidates = [i for i in range(count - 1) if counts[i] < reach]
        whole, remaining = sum([portions[i] for i in candidates]), surplus
        for i in candidates:
            extra = min(reach - counts[i], max(1, remaining * portions[i] // whole), surplus)
            counts[i] = counts[i] + extra
            surplus = surplus - extra
    return np.array([reach] + counts)


def uneven(stream_key, count, total, most, slope):
    if count == 2:
        one = jax.random.randint(stream_key, (), max(1, total - most), min(most, total - 1) + 1)
        return jnp.stack([one, total - one])
    tallies = jnp.asarray(split_up(count, total, most, slope), jnp.int32)
    pairs = (count - 1) // 2
    source_of, sink = tallies[1:1 + 2 * pairs:2], tallies[2:2 + 2 * pairs:2]
    slack = jnp.minimum(source_of - 1, most - sink)
    passed = jax.random.randint(jax.random.fold_in(stream_key, 1), (pairs,), 0, 1 << 20) % (slack + 1)
    tallies = tallies.at[1:1 + 2 * pairs:2].set(source_of - passed).at[2:2 + 2 * pairs:2].set(sink + passed)
    return tallies[jax.random.permutation(jax.random.fold_in(stream_key, 2), count)]


def scatter_about(own_key, shape, deviation, bound, shards=(), kind=jnp.bfloat16):
    drawn = deviation * jax.random.normal(own_key, shape, jnp.float32)
    if shards:
        drawn = drawn * steps_of(own_key, shape, shards, -0.22, 0.18)
    return jnp.clip(drawn, -bound, bound).astype(kind)


def setup_inputs(seed: int = 0) -> dict:
    arg_keys = jax.random.split(jax.random.key(seed), 14)
    return {
        "tokens": scatter_about(arg_keys[0], (ROWS, SEQ, D), 1.0, 6.0, ((1, 32),)),
        "lengths": jax.vmap(lambda own: uneven(own, NDOC, SEQ, 7 * SEQ // 8, 2))(jax.random.split(arg_keys[1], ROWS)).reshape((ROWS, NDOC)).astype(jnp.int32),
        "w_in": scatter_about(arg_keys[2], (2, 3, D, D), D ** -0.5, 0.21875, ((3, 2),)),
        "b_in": scatter_about(arg_keys[3], (2, 2, D), 0.3, 4.0, ((2, 2),)),
        "w_out": scatter_about(arg_keys[4], (2, D, D), (D // 8) ** -0.5, 0.625, ((1, 2),)),
        "w_up": scatter_about(arg_keys[5], (2, D, FF), D ** -0.5, 0.21875, ((2, 2),)),
        "b_up": scatter_about(arg_keys[6], (2, FF), 0.3, 4.0, ((1, 2),)),
        "w_down": scatter_about(arg_keys[7], (2, FF, D), FF ** -0.5, 0.109375, ((1, 2),)),
        "norm_gain": jnp.clip(1.0 + 0.1 * jax.random.normal(arg_keys[8], (2, 2, D), jnp.float32), 0.5, 1.5),
        "norm_bias": scatter_about(arg_keys[9], (2, 4, D), 0.3, 4.0, (), jnp.float32),
        "rel_table": scatter_about(arg_keys[10], (2, HEADS, SEQ), 1.0, 6.0, ((1, 2),), jnp.float32),
        "d_pooled": scatter_about(arg_keys[11], (ROWS, POOLED, D), 1.0, 6.0, ((1, 32),)),
        "d_skip": scatter_about(arg_keys[12], (ROWS, SEQ, D), 1.0, 6.0, ((1, 32),)),
    }


EPS = 1e-06

@jax.custom_vjp
def low(v):
    return lax.optimization_barrier(v.astype(jnp.bfloat16)).astype(jnp.float32)

@jax.custom_vjp
def low_back(v):
    return v

def low_keep(v):
    return (low(v), None)

def low_pass(kept, grad):
    return (grad,)

def back_keep(v):
    return (v, None)

def back_low(kept, grad):
    return (low(grad),)
low.defvjp(low_keep, low_pass)
low_back.defvjp(back_keep, back_low)

def matmul(left, right):
    return jnp.dot(left, right, precision=lax.Precision.HIGHEST)

def norm_rows(values, gain, shift):
    center = values - lax.optimization_barrier(jnp.mean(values, axis=-1, keepdims=True))
    spread = lax.optimization_barrier(jnp.mean(center * center, axis=-1, keepdims=True))
    return center * lax.rsqrt(spread + EPS) * gain + shift

def attention(queries, keys, w_q, w_k, w_v, b_q, b_v, w_o, table, query_documents, key_documents, stride):
    count_q = queries.shape[0]
    count_k = keys.shape[0]
    heads = table.shape[0]
    query = low(low_back(matmul(queries, w_q) + b_q)).reshape(count_q, heads, HEAD_DIM)
    key = low(low_back(matmul(keys, w_k))).reshape(count_k, heads, HEAD_DIM)
    value = low(low_back(matmul(keys, w_v) + b_v)).reshape(count_k, heads, HEAD_DIM)
    offset = jnp.arange(count_k, dtype=jnp.int32)[None, :] - stride * jnp.arange(count_q, dtype=jnp.int32)[:, None] + SEQ // 2
    offset = jnp.clip(offset, 0, SEQ - 1)
    scores = jnp.einsum('qhd,khd->hqk', query, key, precision=lax.Precision.HIGHEST) * HEAD_DIM ** (-0.5)
    scores = low_back(scores + jnp.take(table, offset, axis=1))
    same = query_documents[:, None] == key_documents[None, :]
    scores = jnp.where(same[None], scores, -1e+30)
    shifted = jnp.exp(scores - lax.optimization_barrier(jnp.max(scores, axis=-1, keepdims=True)))
    probs = low(shifted / lax.optimization_barrier(jnp.sum(shifted, axis=-1, keepdims=True)))
    mixed = jnp.einsum('hqk,khd->qhd', probs, value, precision=lax.Precision.HIGHEST)
    mixed = low(low_back(mixed.reshape(count_q, heads * HEAD_DIM)))
    return matmul(mixed, w_o)

def feed(middle, w_up, b_up, w_down):
    upward = low_back(matmul(middle, w_up) + b_up)
    active = low(jax.nn.gelu(upward, approximate=False))
    return matmul(active, w_down)

def block(queries, keys, resid, query_documents, key_documents, stride, layer, params):
    w_in, b_in, w_out, w_up, b_up, w_down, gains, shifts, rel = params
    mixing = low_back(attention(queries, keys, w_in[layer, 0], w_in[layer, 1], w_in[layer, 2], b_in[layer, 0], b_in[layer, 1], w_out[layer], rel[layer], query_documents, key_documents, stride))
    middle = norm_rows(mixing + shifts[layer, 0] + resid, gains[layer, 0], shifts[layer, 1])
    hidden_sum = low_back(feed(low(middle), w_up[layer], b_up[layer], w_down[layer]))
    return norm_rows(hidden_sum + shifts[layer, 2] + middle, gains[layer, 1], shifts[layer, 3])

def pool_pairs(values):
    pairs = values.reshape(values.shape[0] // 2, 2, values.shape[1])
    return 0.5 * (pairs[:, 0] + pairs[:, 1])

def segments(lengths):
    ends = jnp.cumsum(lengths)
    places = jnp.arange(SEQ, dtype=jnp.int32)
    return lax.optimization_barrier(jnp.sum((ends[None, :] <= places[:, None]).astype(jnp.int32), axis=1))

def row_forward(xrow, documents, params):
    pooled_documents = documents.reshape(-1, 2)[:, 0]
    inputs = low_back(xrow)
    pooled = pool_pairs(inputs)
    first = block(low(pooled), low(inputs), pooled, pooled_documents, documents, 2, 0, params)
    first_sent = low(low_back(first))
    second = block(first_sent, first_sent, first_sent, pooled_documents, pooled_documents, 1, 1, params)
    second_out = low(low_back(second))
    skip = xrow + jnp.repeat(second_out, 2, axis=0)
    return (second_out, skip)

def reference(tokens, lengths, w_in, b_in, w_out, w_up, b_up, w_down, norm_gain, norm_bias, rel_table, d_pooled, d_skip):
    documents = jax.vmap(segments)(lengths)
    inputs = tokens.astype(jnp.float32)
    weights = (w_in.astype(jnp.float32), b_in.astype(jnp.float32), w_out.astype(jnp.float32), w_up.astype(jnp.float32), b_up.astype(jnp.float32), w_down.astype(jnp.float32), norm_gain.astype(jnp.float32), norm_bias.astype(jnp.float32), rel_table.astype(jnp.float32))

    def forward(values, *params):

        def one_row(pair):
            return row_forward(pair[0], pair[1], params)
        return lax.map(jax.checkpoint(one_row), (values, documents))
    (second, skip), pull = jax.vjp(forward, inputs, *weights)
    grads = pull((d_pooled.astype(jnp.float32), d_skip.astype(jnp.float32)))
    return (second.astype(jnp.bfloat16), skip.astype(jnp.bfloat16), grads[0].astype(jnp.bfloat16), grads[1], grads[2], grads[3], grads[4], grads[5], grads[6], grads[7], grads[8], grads[9])
```

```python
import functools

import jax
import jax.numpy as jnp
from jax import lax
from jax.experimental import pallas as pl
from jax.experimental.pallas import tpu as pltpu
from jax.sharding import PartitionSpec as P

EPS = 1e-06
LANES = 128
BF = jnp.bfloat16
F32 = jnp.float32
VMEM_LIMIT = 56 * 1024 * 1024
ORDERS = ("xy", "yx")
ROW_BLOCK = 32


def dot(left, right):
    return lax.dot_general(left, right, (((1,), (0,)), ((), ())), preferred_element_type=F32)


def dot_nt(left, right):
    return lax.dot_general(left, right, (((1,), (1,)), ((), ())), preferred_element_type=F32)


def dot_tn(left, right):
    return lax.dot_general(left, right, (((0,), (0,)), ((), ())), preferred_element_type=F32)


def pool_matrix(count):
    place = lax.broadcasted_iota(jnp.int32, (count // 2, count), 0)
    token = lax.broadcasted_iota(jnp.int32, (count // 2, count), 1)
    return jnp.where((token >> 1) == place, 0.5, 0.0).astype(BF)


def spread_matrix(count):
    place = lax.broadcasted_iota(jnp.int32, (count, count // 2), 1)
    token = lax.broadcasted_iota(jnp.int32, (count, count // 2), 0)
    return jnp.where((token >> 1) == place, 0.5, 0.0).astype(BF)


def head_mask(width, head_dim, head, value):
    lane = lax.broadcasted_iota(jnp.int32, (1, width), 1)
    return jnp.where(lane // head_dim == head, value, 0.0).astype(BF)


def blocks(count, size):
    return [slice(at, at + size) for at in range(0, count, size)]


def norm_forward(total, n_out, rate_out):
    for here in blocks(n_out.shape[0], ROW_BLOCK):
        values = total(here)
        center = values - jnp.mean(values, axis=-1, keepdims=True)
        spread = jnp.mean(center * center, axis=-1, keepdims=True)
        rate = lax.rsqrt(spread + EPS)
        n_out[here, :] = center * rate
        rate_out[here, :] = jnp.broadcast_to(rate, (ROW_BLOCK, rate_out.shape[1]))


def norm_backward(grad, normed, rates, gain, put):
    sums = [jnp.zeros((1, normed.shape[1]), F32) for _ in range(3)]
    for here in blocks(normed.shape[0], ROW_BLOCK):
        values, unit = grad[here, :].astype(F32), normed[here, :]
        scaled = values * gain
        mean_one = jnp.mean(scaled, axis=-1, keepdims=True)
        mean_two = jnp.mean(scaled * unit, axis=-1, keepdims=True)
        back = (scaled - mean_one - unit * mean_two) * rates[here, 0:1]
        put(here, back)
        for number, part in enumerate((values * unit, values, back)):
            sums[number] = sums[number] + jnp.sum(part, axis=0, keepdims=True)
    return sums


def row_documents(ends_ref, row, count_q, count_k, step_q, step_k):
    at_q = lax.broadcasted_iota(jnp.int32, (count_q, 1), 0) * step_q
    at_k = lax.broadcasted_iota(jnp.int32, (1, count_k), 1) * step_k
    doc_q = jnp.zeros((count_q, 1), jnp.int32)
    doc_k = jnp.zeros((1, count_k), jnp.int32)
    for number in range(ends_ref.shape[1]):
        end = ends_ref[row, number]
        doc_q = doc_q + (at_q >= end).astype(jnp.int32)
        doc_k = doc_k + (at_k >= end).astype(jnp.int32)
    return doc_q, doc_k


def fill_bias(bias_ref, head, table_row, stride):
    count_q, count_k = bias_ref.shape[1:]
    span = table_row.shape[1]
    base = jnp.concatenate([pltpu.roll(table_row, stride * low, 1) for low in range(8)], axis=0)
    step = 8 * stride
    for turn in range(LANES // step):
        back = (span // 2 - step * turn) % LANES
        rolled = pltpu.roll(base, (span - back) % span, 1)
        for block in range(turn, count_q // 8, LANES // step):
            at = span // 2 - step * block - back
            bias_ref[head, 8 * block : 8 * block + 8, :] = rolled[:, at : at + count_k]


def unroll_sum(block_values, count_q, count_k, span, stride):
    total = jnp.zeros((8, span), F32)
    step = 8 * stride
    for turn in range(LANES // step):
        back = (span // 2 - step * turn) % LANES
        part = jnp.zeros((8, span), F32)
        for block in range(turn, count_q // 8, LANES // step):
            at = span // 2 - step * block - back
            columns = [block_values(block)]
            if at:
                columns = [jnp.zeros((8, at), F32)] + columns
            if span - at - count_k:
                columns = columns + [jnp.zeros((8, span - at - count_k), F32)]
            part = part + jnp.concatenate(columns, axis=1)
        total = total + pltpu.roll(part, back, 1)
    out = total[0:1]
    for low in range(1, 8):
        out = out + pltpu.roll(total[low : low + 1], (span - stride * low) % span, 1)
    return out


def with_extras(kernel, count):
    def run(*refs, inputs):
        return kernel(*refs[:inputs], *refs[inputs + count :])

    return run


def call(kernel, in_specs, operands, after=(), **kwargs):
    if after:
        body = functools.partial(with_extras(kernel, len(after)), inputs=len(operands))
        in_specs = list(in_specs) + [pl.BlockSpec(memory_space=pl.ANY)] * len(after)
    else:
        body = kernel
    return pl.pallas_call(body, in_specs=in_specs, **kwargs)(*operands, *after)


def attend_forward_kernel(
    pooling, rows, heads, head_dim,
    ends_ref, x_ref, wi_a, wi_b, bias_in_ref, wo_a, wo_b, tab_ref, shift_ref,
    q_out, k_out, v_out, p_out, mix_out, n_out, rate_out,
    acc_ref, bias_ref, query_ref, score_ref, *resid_ref,
):
    step = pl.program_id(0)
    last = pl.num_programs(0) - 1
    count_k = x_ref.shape[1]
    count_q = acc_ref.shape[0] // rows
    width = x_ref.shape[2]
    group = heads * head_dim
    stride = 2 if pooling else 1

    @pl.when(step == 0)
    def _():
        if pooling:
            pool = pool_matrix(count_k)
            for row in range(rows):
                pooled = dot(pool, x_ref[row])
                resid_ref[0][row * count_q : (row + 1) * count_q, :] = pooled
                query_ref[row * count_q : (row + 1) * count_q, :] = pooled.astype(BF)
        else:
            query_ref[...] = x_ref[...].reshape(rows * count_q, width)
        acc_ref[...] = jnp.zeros_like(acc_ref)

    x = x_ref[...].reshape(rows * count_k, width)
    wq = jnp.concatenate([wi_a[0], wi_b[0]], axis=1)
    wk = jnp.concatenate([wi_a[1], wi_b[1]], axis=1)
    wv = jnp.concatenate([wi_a[2], wi_b[2]], axis=1)
    query = (dot(query_ref[...], wq) + bias_in_ref[0:1, :]).astype(BF)
    key = dot(x, wk).astype(BF)
    value = (dot(x, wv) + bias_in_ref[1:2, :]).astype(BF)
    q_out[...] = query
    k_out[...] = key
    v_out[...] = value
    for head in range(heads):
        fill_bias(bias_ref, head, tab_ref[head : head + 1, :], stride)
    lane = lax.broadcasted_iota(jnp.int32, (1, group), 1) // head_dim
    for row in range(rows):
        q_row = query[row * count_q : (row + 1) * count_q]
        masked = [q_row * head_mask(group, head_dim, head, head_dim ** (-0.5)) for head in range(heads)]
        score_ref[row] = dot_nt(jnp.concatenate(masked, axis=0), key[row * count_k : (row + 1) * count_k])
    for row in range(rows):
        doc_q, doc_k = row_documents(ends_ref, row, count_q, count_k, 2, 2 // stride)
        for head in range(heads):
            for here in blocks(count_q, ROW_BLOCK):
                at = slice(head * count_q + here.start, head * count_q + here.stop)
                same = doc_q[here] == doc_k
                scores = jnp.where(same, score_ref[row, at, :] + bias_ref[head, here, :], -1e30)
                top = jnp.max(scores, axis=-1, keepdims=True)
                expo = jnp.exp(scores - top)
                denom = jnp.sum(expo, axis=-1, keepdims=True)
                p_out[row, at, :] = (expo * (1.0 / denom)).astype(BF)
    for row in range(rows):
        every = dot(p_out[row], value[row * count_k : (row + 1) * count_k])
        mixed = every[:count_q]
        for head in range(1, heads):
            mixed = jnp.where(lane == head, every[head * count_q : (head + 1) * count_q], mixed)
        mix_out[row * count_q : (row + 1) * count_q, :] = mixed.astype(BF)
    wo = jnp.concatenate([wo_a[...], wo_b[...]], axis=0)
    acc_ref[...] += dot(mix_out[...], wo)

    @pl.when(step == last)
    def _():

        def total_of(here):
            resid = resid_ref[0][here, :] if pooling else query_ref[here, :].astype(F32)
            return acc_ref[here, :] + shift_ref[0:1, :] + resid

        norm_forward(total_of, n_out, rate_out)


def feed_forward_kernel(
    n_ref, gain_ref, shift_ref, wu_a, wu_b, bu_ref, wd_a, wd_b,
    act_out, dg_out, res_out, n_out, rate_out,
    mid_ref, acc_ref, up_ref,
):
    step = pl.program_id(0)
    last = pl.num_programs(0) - 1
    tile = wu_a.shape[1]

    @pl.when(step == 0)
    def _():
        middle = n_ref[...] * gain_ref[0:1, :] + shift_ref[1:2, :]
        mid_ref[...] = middle.astype(BF)
        acc_ref[...] = middle + shift_ref[2:3, :]

    for number, wu in enumerate((wu_a, wu_b)):
        up_ref[number] = dot(mid_ref[...], wu[...])
    for number in range(2):
        cols = slice(number * tile, (number + 1) * tile)
        for here in blocks(up_ref.shape[1], ROW_BLOCK):
            up = up_ref[number, here, :] + bu_ref[:, cols]
            cdf = 0.5 * (1.0 + lax.erf(up * (0.5**0.5)))
            density = jnp.exp(up * up * (-0.5)) * 0.3989422804014327
            dg_out[here, cols] = (cdf + up * density).astype(BF)
            act_out[here, cols] = (up * cdf).astype(BF)
    acc_ref[...] += dot(act_out[:, :tile], wd_a[...]) + dot(act_out[:, tile:], wd_b[...])

    @pl.when(step == last)
    def _():
        norm_forward(lambda here: acc_ref[here, :], n_out, rate_out)
        res_out[...] = (n_out[...] * gain_ref[1:2, :] + shift_ref[3:4, :]).astype(BF)


def feed_backward_kernel(
    grad_ref, n2_ref, rate2_ref, n1_ref, rate1_ref, gain_ref, shift_ref, act_ref, dg_ref, wu_a, wu_b, wd_a, wd_b,
    gwu_a, gwu_b, gwd_a, gwd_b, gbu_out, att_out, resid_out, small_out,
    down_ref, mid_t_ref, acc_ref, up_ref,
):
    step = pl.program_id(0)
    last = pl.num_programs(0) - 1
    tile = wu_a.shape[1]

    @pl.when(step == 0)
    def _():

        def put(here, back):
            down_ref[here, :] = back.astype(BF)
            acc_ref[here, :] = back

        row_gain, row_shift, row_out = norm_backward(grad_ref, n2_ref, rate2_ref, gain_ref[1:2, :], put)
        small_out[...] = jnp.zeros_like(small_out)
        small_out[1:2, :] = row_gain
        small_out[4:5, :] = row_out
        small_out[5:6, :] = row_shift
        middle = (n1_ref[...] * gain_ref[0:1, :] + shift_ref[1:2, :]).astype(BF)
        mid_t_ref[...] = middle.T

    for number, (wd, gwd) in enumerate(((wd_a, gwd_a), (wd_b, gwd_b))):
        cols = slice(number * tile, (number + 1) * tile)
        grad_act = dot_nt(down_ref[...], wd[...])
        gwd[...] = dot_tn(act_ref[:, cols], down_ref[...]).astype(BF)
        summed = jnp.zeros((1, tile), F32)
        for here in blocks(grad_act.shape[0], ROW_BLOCK):
            grad_up = (grad_act[here] * dg_ref[here, cols].astype(F32)).astype(BF)
            up_ref[here, cols] = grad_up
            summed = summed + jnp.sum(grad_up.astype(F32), axis=0, keepdims=True)
        gbu_out[:, cols] = summed
    gwu_a[...] = dot(mid_t_ref[...], up_ref[:, :tile]).astype(BF)
    gwu_b[...] = dot(mid_t_ref[...], up_ref[:, tile:]).astype(BF)
    acc_ref[...] += dot_nt(up_ref[:, :tile], wu_a[...]) + dot_nt(up_ref[:, tile:], wu_b[...])

    @pl.when(step == last)
    def _():

        def put(here, back):
            att_out[here, :] = back.astype(BF)
            resid_out[here, :] = back

        row_gain, row_shift, row_out = norm_backward(acc_ref, n1_ref, rate1_ref, gain_ref[0:1, :], put)
        small_out[0:1, :] = row_gain
        small_out[2:3, :] = row_out
        small_out[3:4, :] = row_shift


def attend_backward_kernel(
    pooling, rows, heads, head_dim,
    att_ref, resid_ref, x_ref, q_ref, k_ref, v_ref, p_ref, mix_ref, wi_a, wi_b, wo_a, wo_b,
    g_a, g_b, gb_out, tab_out, in_out,
    x_t_ref, query_t_ref, att_t_ref, acc_k_ref, acc_q_ref, ds_ref, dp_ref, dom_ref, qm_ref, dq_ref, dkv_ref,
):
    step = pl.program_id(0)
    last = pl.num_programs(0) - 1
    count_k = x_ref.shape[1]
    count_q = att_ref.shape[0] // rows
    width = x_ref.shape[2]
    group = heads * head_dim
    stride = 2 if pooling else 1
    span = tab_out.shape[1]

    @pl.when(step == 0)
    def _():
        x = x_ref[...].reshape(rows * count_k, width)
        x_t_ref[...] = x.T
        if pooling:
            pool = pool_matrix(count_k)
            for row in range(rows):
                query_t_ref[:, row * count_q : (row + 1) * count_q] = dot(pool, x_ref[row]).astype(BF).T
        att_t_ref[...] = att_ref[...].T
        if pooling:
            acc_k_ref[...] = jnp.zeros_like(acc_k_ref)
            acc_q_ref[...] = resid_ref[...]
        else:
            acc_k_ref[...] = resid_ref[...]

    wo = jnp.concatenate([wo_a[...], wo_b[...]], axis=0)
    grad_mixed = dot_nt(att_ref[...], wo).astype(BF)
    lane = lax.broadcasted_iota(jnp.int32, (1, group), 1) // head_dim
    for row in range(rows):
        q_row = q_ref[row * count_q : (row + 1) * count_q, :]
        g_row = grad_mixed[row * count_q : (row + 1) * count_q]
        for head in range(heads):
            at = slice(head * count_q, (head + 1) * count_q)
            dom_ref[row, at, :] = g_row * head_mask(group, head_dim, head, 1.0)
            qm_ref[row, at, :] = q_row * head_mask(group, head_dim, head, head_dim ** (-0.5))
        dp_ref[row] = dot_nt(dom_ref[row], v_ref[row * count_k : (row + 1) * count_k, :])
    for row in range(rows):
        for at in blocks(heads * count_q, ROW_BLOCK):
            probs = p_ref[row, at, :].astype(F32)
            terms = probs * dp_ref[row, at, :]
            ds_ref[row, at, :] = (terms - probs * jnp.sum(terms, axis=-1, keepdims=True)).astype(BF)
    for row in range(rows):
        keys = slice(row * count_k, (row + 1) * count_k)
        every = dot(ds_ref[row], k_ref[keys, :])
        grad_q = every[:count_q]
        for head in range(1, heads):
            grad_q = jnp.where(lane == head, every[head * count_q : (head + 1) * count_q], grad_q)
        dq_ref[row * count_q : (row + 1) * count_q, :] = (grad_q * head_dim ** (-0.5)).astype(BF)
        dkv_ref[keys, :group] = dot_tn(ds_ref[row], qm_ref[row]).astype(BF)
        dkv_ref[keys, group:] = dot_tn(p_ref[row], dom_ref[row]).astype(BF)
    for head in range(heads):


        def block_values(block, first=head * count_q):
            at = slice(first + 8 * block, first + 8 * block + 8)
            return functools.reduce(jnp.add, [ds_ref[row, at, :].astype(F32) for row in range(rows)])

        tab_out[head : head + 1, :] = unroll_sum(block_values, count_q, count_k, span, stride)
    half = group // 2
    query_t = query_t_ref[...] if pooling else x_t_ref[...]
    grad_wq = dot(query_t, dq_ref[...]).astype(BF)
    grad_wk = dot(x_t_ref[...], dkv_ref[:, :group]).astype(BF)
    grad_wv = dot(x_t_ref[...], dkv_ref[:, group:]).astype(BF)
    grad_wo = dot(att_t_ref[...], mix_ref[...]).astype(BF)
    for slot, grad in enumerate((grad_wq, grad_wk, grad_wv, grad_wo)):
        g_a[slot] = grad[:, :half]
        g_b[slot] = grad[:, half:]
    gb_out[0:1, :] = jnp.sum(dq_ref[...].astype(F32), axis=0, keepdims=True)
    gb_out[1:2, :] = jnp.sum(dkv_ref[:, group:].astype(F32), axis=0, keepdims=True)
    wq = jnp.concatenate([wi_a[0], wi_b[0]], axis=1)
    wkv = jnp.concatenate([wi_a[1], wi_b[1], wi_a[2], wi_b[2]], axis=1)
    if pooling:
        acc_q_ref[...] += dot_nt(dq_ref[...], wq)
        acc_k_ref[...] += dot_nt(dkv_ref[...], wkv)
    else:
        acc_k_ref[...] += dot_nt(dq_ref[...], wq) + dot_nt(dkv_ref[...], wkv)

    @pl.when(step == last)
    def _():
        if pooling:
            spread = spread_matrix(count_k)
            for row in range(rows):
                total = acc_q_ref[row * count_q : (row + 1) * count_q, :]
                high = total.astype(BF)
                rest = (total - high.astype(F32)).astype(BF)
                keys = slice(row * count_k, (row + 1) * count_k)
                back = (acc_k_ref[keys, :] + dot(spread, high) + dot(spread, rest)).astype(BF)
                if len(in_out.shape) == 2:
                    in_out[keys, :] = back
                else:
                    in_out[:, row] = back.reshape(in_out.shape[0], *in_out.shape[2:])
        else:
            in_out[...] = acc_k_ref[...].astype(BF)


def whole(shape):
    return pl.BlockSpec(shape, lambda step: (0,) * len(shape))


def params():
    return pltpu.CompilerParams(dimension_semantics=("arbitrary",), vmem_limit_bytes=VMEM_LIMIT)


def cost(flops, arrays, transcendentals=0):
    moved = sum(array.size * array.dtype.itemsize for array in arrays)
    return pl.CostEstimate(flops=int(flops), bytes_accessed=int(moved), transcendentals=int(transcendentals))


def sds(shape, dtype):
    return jax.ShapeDtypeStruct(shape, dtype)


def attend_forward(layer, x, ends, own, other, small, shift):
    rows, count_k, width = x.shape
    pooling = layer == 0
    count_q = count_k // 2 if pooling else count_k
    wi_a, wo_a, wi_b, wo_b = own["w_in"], own["w_out"], other["w_in"], other["w_out"]
    local = wi_a.shape[3]
    steps = local // LANES
    head_dim = small["head_dim"]
    heads = 2 * LANES // head_dim
    group = 2 * LANES
    flat_q, flat_k = rows * count_q, rows * count_k
    table = small["table"][layer]
    span = table.shape[2]
    weight = pl.BlockSpec((None, 3, width, LANES), lambda step: (layer, 0, 0, step))
    out_w = pl.BlockSpec((None, LANES, width), lambda step: (layer, step, 0))
    out_shape = (
        sds((steps, flat_q, group), BF),
        sds((steps, flat_k, group), BF),
        sds((steps, flat_k, group), BF),
        sds((steps, rows, heads * count_q, count_k), BF),
        sds((steps, flat_q, group), BF),
        sds((flat_q, width), F32),
        sds((flat_q, LANES), F32),
    )
    scratch = [
        pltpu.VMEM((flat_q, width), F32),
        pltpu.VMEM((heads, count_q, count_k), F32),
        pltpu.VMEM((flat_q, width), BF),
        pltpu.VMEM((rows, heads * count_q, count_k), F32),
    ]
    if pooling:
        scratch.append(pltpu.VMEM((flat_q, width), F32))
    macs = (2 * flat_q + 2 * flat_k) * width * width + 2 * steps * group * flat_q * count_k * heads
    return pl.pallas_call(
        functools.partial(attend_forward_kernel, pooling, rows, heads, head_dim),
        grid=(steps,),
        in_specs=[
            pl.BlockSpec(memory_space=pltpu.SMEM),
            whole((rows, count_k, width)),
            weight,
            weight,
            pl.BlockSpec((None, 2, group), lambda step: (step, 0, 0)),
            out_w,
            out_w,
            pl.BlockSpec((None, heads, span), lambda step: (step, 0, 0)),
            whole(shift.shape),
        ],
        out_specs=[
            pl.BlockSpec((None, flat_q, group), lambda step: (step, 0, 0)),
            pl.BlockSpec((None, flat_k, group), lambda step: (step, 0, 0)),
            pl.BlockSpec((None, flat_k, group), lambda step: (step, 0, 0)),
            pl.BlockSpec((None, rows, heads * count_q, count_k), lambda step: (step, 0, 0, 0)),
            pl.BlockSpec((None, flat_q, group), lambda step: (step, 0, 0)),
            whole((flat_q, width)),
            whole((flat_q, LANES)),
        ],
        out_shape=out_shape,
        scratch_shapes=scratch,
        compiler_params=params(),
        cost_estimate=cost(2 * macs, out_shape, steps * heads * flat_q * count_k),
        name=f"attend_forward_{layer}",
    )(ends, x, wi_a, wi_b, small["b_in"][layer], wo_a, wo_b, table, shift)


def feed_forward(layer, normed, own, other, small, gain, shift):
    flat, width = normed.shape
    wu_a, wd_a, wu_b, wd_b = own["w_up"], own["w_down"], other["w_up"], other["w_down"]
    bias = small["b_up"][layer]
    steps, _, both = bias.shape
    tile = both // 2
    up_w = pl.BlockSpec((None, width, tile), lambda step: (layer, 0, step))
    down_w = pl.BlockSpec((None, tile, width), lambda step: (layer, step, 0))
    wide = pl.BlockSpec((None, flat, both), lambda step: (step, 0, 0))
    out_shape = (
        sds((steps, flat, both), BF),
        sds((steps, flat, both), BF),
        sds((flat, width), BF),
        sds((flat, width), F32),
        sds((flat, LANES), F32),
    )
    return pl.pallas_call(
        feed_forward_kernel,
        grid=(steps,),
        in_specs=[
            whole((flat, width)),
            whole(gain.shape),
            whole(shift.shape),
            up_w,
            up_w,
            pl.BlockSpec((None, 1, both), lambda step: (step, 0, 0)),
            down_w,
            down_w,
        ],
        out_specs=[wide, wide, whole((flat, width)), whole((flat, width)), whole((flat, LANES))],
        out_shape=out_shape,
        scratch_shapes=[
            pltpu.VMEM((flat, width), BF),
            pltpu.VMEM((flat, width), F32),
            pltpu.VMEM((2, flat, tile), F32),
        ],
        compiler_params=params(),
        cost_estimate=cost(4 * flat * width * steps * both, out_shape, 2 * flat * steps * both),
        name=f"feed_forward_{layer}",
    )(normed, gain, shift, wu_a, wu_b, bias, wd_a, wd_b)


def feed_backward(layer, grad, kept, own, other, small, gain, shift, after=()):
    normed2, rate2, normed1, rate1, act, dg = kept
    flat, width = normed1.shape
    wu_a, wd_a, wu_b, wd_b = own["w_up"], own["w_down"], other["w_up"], other["w_down"]
    steps, _, both = act.shape
    tile = both // 2
    units = steps * tile
    up_w = pl.BlockSpec((None, width, tile), lambda step: (layer, 0, step))
    down_w = pl.BlockSpec((None, tile, width), lambda step: (layer, step, 0))
    up_g = pl.BlockSpec((width, tile), lambda step: (0, step))
    down_g = pl.BlockSpec((tile, width), lambda step: (step, 0))
    wide = pl.BlockSpec((None, flat, both), lambda step: (step, 0, 0))
    out_shape = (
        sds((width, units), BF),
        sds((width, units), BF),
        sds((units, width), BF),
        sds((units, width), BF),
        sds((steps, 1, both), F32),
        sds((flat, width), BF),
        sds((flat, width), F32),
        sds((8, width), F32),
    )
    return call(
        feed_backward_kernel,
        grid=(steps,),
        operands=(grad, normed2, rate2, normed1, rate1, gain, shift, act, dg, wu_a, wu_b, wd_a, wd_b),
        after=after,
        in_specs=[
            whole((flat, width)),
            whole((flat, width)),
            whole((flat, LANES)),
            whole((flat, width)),
            whole((flat, LANES)),
            whole(gain.shape),
            whole(shift.shape),
            wide,
            wide,
            up_w,
            up_w,
            down_w,
            down_w,
        ],
        out_specs=[
            up_g,
            up_g,
            down_g,
            down_g,
            pl.BlockSpec((None, 1, both), lambda step: (step, 0, 0)),
            whole((flat, width)),
            whole((flat, width)),
            whole((8, width)),
        ],
        out_shape=out_shape,
        scratch_shapes=[
            pltpu.VMEM((flat, width), BF),
            pltpu.VMEM((width, flat), BF),
            pltpu.VMEM((flat, width), F32),
            pltpu.VMEM((flat, both), BF),
        ],
        compiler_params=params(),
        cost_estimate=cost(8 * flat * width * steps * both, out_shape + (act, dg)),
        name=f"feed_backward_{layer}",
    )


def attend_backward(layer, grad_att, grad_resid, x, kept, own, other, small, after=(), places=0):
    rows, count_k, width = x.shape
    pooling = layer == 0
    count_q = count_k // 2 if pooling else count_k
    query, key, value, probs, mixed = kept
    wi_a, wo_a, wi_b, wo_b = own["w_in"], own["w_out"], other["w_in"], other["w_out"]
    local = wi_a.shape[3]
    steps = local // LANES
    head_dim = small["head_dim"]
    heads = 2 * LANES // head_dim
    group = 2 * LANES
    flat_q, flat_k = rows * count_q, rows * count_k
    span = small["table"][layer].shape[2]
    weight = pl.BlockSpec((None, 3, width, LANES), lambda step: (layer, 0, 0, step))
    out_w = pl.BlockSpec((None, LANES, width), lambda step: (layer, step, 0))
    grad_w = pl.BlockSpec((4, width, LANES), lambda step: (0, 0, step))
    by_q = pl.BlockSpec((None, flat_q, group), lambda step: (step, 0, 0))
    by_k = pl.BlockSpec((None, flat_k, group), lambda step: (step, 0, 0))
    out_shape = (
        sds((4, width, local), BF),
        sds((4, width, local), BF),
        sds((steps, 2, group), F32),
        sds((steps, heads, span), F32),
        sds((places, rows, count_k // places, width) if places else (flat_k, width), BF),
    )
    macs = 2 * (2 * flat_q + 2 * flat_k) * width * width + 5 * steps * group * flat_q * count_k * heads
    return call(
        functools.partial(attend_backward_kernel, pooling, rows, heads, head_dim),
        grid=(steps,),
        operands=(grad_att, grad_resid, x, query, key, value, probs, mixed, wi_a, wi_b, wo_a, wo_b),
        after=after,
        in_specs=[
            whole((flat_q, width)),
            whole((flat_q, width)),
            whole((rows, count_k, width)),
            by_q,
            by_k,
            by_k,
            pl.BlockSpec((None, rows, heads * count_q, count_k), lambda step: (step, 0, 0, 0)),
            by_q,
            weight,
            weight,
            out_w,
            out_w,
        ],
        out_specs=[
            grad_w,
            grad_w,
            pl.BlockSpec((None, 2, group), lambda step: (step, 0, 0)),
            pl.BlockSpec((None, heads, span), lambda step: (step, 0, 0)),
            whole(out_shape[4].shape),
        ],
        out_shape=out_shape,
        scratch_shapes=[
            pltpu.VMEM((width, flat_k), BF),
            pltpu.VMEM((width, flat_q) if pooling else (8, LANES), BF),
            pltpu.VMEM((width, flat_q), BF),
            pltpu.VMEM((flat_k, width), F32),
            pltpu.VMEM((flat_q, width) if pooling else (8, LANES), F32),
            pltpu.VMEM((rows, heads * count_q, count_k), BF),
            pltpu.VMEM((rows, heads * count_q, count_k), F32),
            pltpu.VMEM((rows, heads * count_q, group), BF),
            pltpu.VMEM((rows, heads * count_q, group), BF),
            pltpu.VMEM((flat_q, group), BF),
            pltpu.VMEM((flat_k, 2 * group), BF),
        ],
        compiler_params=params(),
        cost_estimate=cost(2 * macs, out_shape + (probs,)),
        name=f"attend_backward_{layer}",
    )


def pair_sum_kernel(skip_ref, pooled_ref, out_ref):
    count = skip_ref.shape[0]
    part = 192
    pool = pool_matrix(part)
    for at in range(0, count, part):
        half = slice(at // 2, (at + part) // 2)
        pair = 2.0 * dot(pool, skip_ref[at : at + part, :])
        out_ref[half, :] = (pooled_ref[half, :].astype(F32) + pair).astype(BF)


def skip_kernel(tokens_ref, skip_ref, pooled_ref, grad_ref, sum_out, grad_out):
    count = tokens_ref.shape[0]
    part = 192
    spread = spread_matrix(part)
    for at in range(0, count, part):
        here = slice(at, at + part)
        again = 2.0 * dot(spread, pooled_ref[at // 2 : (at + part) // 2, :])
        sum_out[here, :] = (tokens_ref[here, :].astype(F32) + again).astype(BF)
        grad_out[here, :] = (skip_ref[here, :].astype(F32) + grad_ref[here, :].astype(F32)).astype(BF)


def plain_call(kernel, out_shape, *arrays):
    return pl.pallas_call(
        kernel,
        out_shape=out_shape,
        compiler_params=pltpu.CompilerParams(vmem_limit_bytes=VMEM_LIMIT),
        cost_estimate=cost(1e9, arrays),
    )(*arrays)


def swap(array):
    return lax.ppermute(array, "head", [(0, 1), (1, 0)])


def grid_sizes(devices):
    bits = devices.bit_length() - 1
    side = 1 << (bits // 3)
    return {"z": devices // (side * side), "y": side, "x": side}


def place_of(index, sizes):
    return {
        "z": index // (sizes["y"] * sizes["x"]),
        "y": (index // sizes["x"]) % sizes["y"],
        "x": index % sizes["x"],
    }


def moved(array, sizes, axis, target):
    count = sizes["z"] * sizes["y"] * sizes["x"]
    pairs = []
    for index in range(count):
        at = place_of(index, sizes)
        at[axis] = target(at[axis]) % sizes[axis]
        pairs.append((index, (at["z"] * sizes["y"] + at["y"]) * sizes["x"] + at["x"]))
    return lax.ppermute(array, "dev", pairs)


def shifted(array, sizes, axis, by):
    return moved(array, sizes, axis, lambda at: at + by)


def lines(sizes, axis):
    count = sizes["z"] * sizes["y"] * sizes["x"]
    found = {}
    for index in range(count):
        at = place_of(index, sizes)
        at[axis] = -1
        found.setdefault(tuple(at.values()), []).append(index)
    return list(found.values())


def pair_sum(array, sizes, axis, step):
    return array + moved(array, sizes, axis, lambda at: at ^ step)


def pair_sum_rest(array, sizes, axis):
    step = 2
    while step < sizes[axis]:
        array = pair_sum(array, sizes, axis, step)
        step *= 2
    return array


def pick(array, number):
    return lax.dynamic_index_in_dim(array, number, 0, keepdims=False)


def total(terms):
    return functools.reduce(jnp.add, [term.astype(F32) for term in terms]).astype(BF)


def tie(*groups):
    leaves, tree = jax.tree.flatten(groups)
    return jax.tree.unflatten(tree, lax.optimization_barrier(leaves))


class Reduction:
    def __init__(self, mine, sizes, place, order, half=0, halves=1):
        self.sizes, self.place, self.order = sizes, place, order + "z"
        self.size = [sizes[axis] for axis in self.order]
        cols = mine.shape[-1]
        rows = mine.size // cols // halves
        self.rows, self.cols = rows // (self.size[0] * self.size[1] * self.size[2]), cols
        self.shape = (halves * self.size[0], *self.size[1:], self.rows, cols)
        self.lead = half * self.size[0]
        self.base = [mine.reshape(self.shape)]
        self.first, self.second = [], []

    def absorb(self, array):
        self.base = self.base + [array.reshape(self.shape)]

    def first_sends(self):
        at, size = self.place[self.order[0]], self.size[0]
        return [total([pick(term, self.lead + (at + by) % size) for term in self.base]) for by in range(1, size)]

    def second_sends(self):
        at = self.lead + self.place[self.order[0]]
        here, size = self.place[self.order[1]], self.size[1]
        sends = []
        for by in range(1, size):
            to = (here + by) % size
            zero = jnp.zeros_like(to)
            corner = (at, to, zero, zero, zero)
            cut = (1, 1, *self.shape[2:])
            terms = [lax.dynamic_slice(term, corner, cut).reshape(self.shape[2:]) for term in self.base]
            sends.append(total(terms + [pick(term, to) for term in self.first]))
        return sends

    def moves(self, level, sends):
        return [shifted(array, self.sizes, self.order[level], by + 1) for by, array in enumerate(sends)]


def packed_rows(reduction):
    return -(-reduction.rows // 16) * 16


def pack_kernel(counts, place_ref, *refs):
    out_ref = refs[-1]
    width = out_ref.shape[1]
    start = at = 0
    for count in counts:
        terms = [ref[...].astype(F32) for ref in refs[start : start + count]]
        start += count
        summed = functools.reduce(jnp.add, terms).astype(BF)
        rows, cols = summed.shape
        for col in range(0, cols, width):
            out_ref[at : at + rows, :] = summed[:, col : col + width]
            at += -(-rows // 16) * 16


def on_tiles(reductions):
    return all(each.rows % 16 == 0 for each in reductions)


def pack_small(reductions, width):
    parts = []
    for each in reductions:
        at, here = each.lead + each.place[each.order[0]], each.place[each.order[1]]
        terms = [pick(pick(term, at), here) for term in each.base] + [pick(term, here) for term in each.first]
        summed = total(terms + each.second)
        for col in range(0, each.cols, width):
            part = summed[:, :, col : col + width]
            parts.append(jnp.pad(part, ((0, 0), (0, packed_rows(each) - each.rows), (0, 0))))
    return jnp.concatenate(parts, axis=1)


def unpack_small(gathered, reductions, sizes):
    width = gathered.shape[2]
    out, at = [], 0
    for each in reductions:
        parts = []
        for _ in range(0, each.cols, width):
            parts.append(gathered[:, at : at + each.rows])
            at += packed_rows(each)
        pieces = jnp.concatenate(parts, axis=2).reshape(
            *[sizes[axis] for axis in "zyx"], each.rows, each.cols
        )
        pieces = pieces.transpose(*["zyx".index(axis) for axis in each.order], 3, 4)
        out.append(pieces.reshape(-1, each.cols).astype(F32))
    return out


def assemble_small(gathered1, gathered10, gathered0, feed1, att1, feed0, att0, sizes):
    up1, down1 = unpack_small(gathered1, feed1, sizes)
    low1, up0, high1, down0 = unpack_small(gathered10, [att1[0], feed0[0], att1[1], feed0[1]], sizes)
    low0, high0 = unpack_small(gathered0, att0, sizes)
    half = high0.shape[0] // 2
    w_in = jnp.stack([jnp.concatenate([low0, high0[:half]]), jnp.concatenate([low1, high1[:half]])])
    w_out = jnp.stack([high0[half:], high1[half:]])
    return jnp.stack([up0, up1]), jnp.stack([down0, down1]), w_in, w_out


def pack(reductions, place):
    width = min(reduction.cols for reduction in reductions)
    line = reductions[0].size[2]
    operands, specs, counts = [], [], []
    axes = {"z": 0, "y": 1, "x": 2}
    if not on_tiles(reductions):
        return pack_small(reductions, width)
    for each in reductions:
        block = (each.rows, each.cols)
        one, two, lead = axes[each.order[0]], axes[each.order[1]], each.lead

        def base_map(step, at, one=one, two=two, lead=lead):
            return (lead + at[one], at[two], step, 0, 0)

        def first_map(step, at, two=two):
            return (at[two], step, 0, 0)

        operands += each.base + each.first + each.second
        specs += [pl.BlockSpec((None, None, None, *block), base_map)] * len(each.base)
        specs += [pl.BlockSpec((None, None, *block), first_map)] * len(each.first)
        specs += [pl.BlockSpec((None, *block), lambda step, at: (step, 0, 0))] * len(each.second)
        counts.append(len(each.base) + len(each.first) + len(each.second))
    rows = sum(packed_rows(each) * (each.cols // width) for each in reductions)
    place_array = jnp.stack([place["z"], place["y"], place["x"]]).astype(jnp.int32)
    return pl.pallas_call(
        functools.partial(pack_kernel, counts),
        grid_spec=pltpu.PrefetchScalarGridSpec(
            num_scalar_prefetch=1,
            grid=(line,),
            in_specs=specs,
            out_specs=pl.BlockSpec((None, rows, width), lambda step, at: (step, 0, 0)),
        ),
        out_shape=sds((line, rows, width), BF),
        compiler_params=params(),
        cost_estimate=cost(0, operands),
        name="pack_quarters",
    )(place_array, *operands)


def along_z(packed, sizes):
    return lax.all_to_all(packed, "dev", 0, 0, axis_index_groups=lines(sizes, "z"), tiled=True)


def line_sum(pieces):
    return total([pieces[number] for number in range(pieces.shape[0])])


def unpack(ref, at, rows, cols):
    width = ref.shape[1]
    parts = []
    for _ in range(0, cols, width):
        parts.append(ref[at : at + rows, :].astype(F32))
        at += -(-rows // 16) * 16
    return (parts[0] if len(parts) == 1 else jnp.concatenate(parts, axis=1)), at


def line_of(piece, sizes):
    return [piece] + [shifted(piece, sizes, "z", by) for by in range(1, sizes["z"])]


def plane_of(line, sizes):
    rows = line[0].shape[0] // 2
    found = []
    for half, (_, second) in enumerate(ORDERS):
        own = jnp.stack([each[half * rows : (half + 1) * rows] for each in line])
        found.append([own] + [shifted(own, sizes, second, by) for by in range(1, sizes[second])])
    return found


def all_of(planes, sizes):
    found = []
    for plane, (first, _) in zip(planes, ORDERS):
        arrays = list(plane)
        for by in range(1, sizes[first]):
            arrays += [shifted(array, sizes, first, by) for array in plane]
        found.append(arrays)
    return found


def put_part(outs, kind, flat, half, source, at):
    if kind in ("up", "down"):
        outs[kind][flat], at = unpack(source, at, *outs[kind].shape[1:])
        return at
    values, at = unpack(source, at, *outs["in"].shape[1:])
    if kind == "low":
        outs["in"][flat] = values
    else:

        @pl.when(flat < half)
        def _():
            outs["in"][2 * half + flat] = values

        @pl.when(flat >= half)
        def _():
            outs["out"][flat - half] = values

    return at


def assemble_kernel(sizes, names, kinds, place_ref, *refs):
    outs = dict(zip(names, refs[len(refs) - len(names) :]))
    axes = {"z": 0, "y": 1, "x": 2}
    start = 0
    for (one, two), wanted in zip(ORDERS, kinds):
        size_a, size_b = sizes[one], sizes[two]
        half = size_a * size_b // 2
        for by_a in range(size_a):
            for by_b in range(size_b):
                source = refs[start]
                start += 1
                at_a = lax.rem(place_ref[axes[one]] + (size_a - by_a), size_a)
                at_b = lax.rem(place_ref[axes[two]] + (size_b - by_b), size_b)
                at = 0
                for kind in wanted:
                    at = put_part(outs, kind, at_a * size_b + at_b, half, source, at)


def assemble(found, kinds, layers, shapes, sizes, place, earlier):
    names = list(layers)
    plane = sizes["x"] * sizes["y"]
    line = sizes["z"]
    counts = {"up": plane, "down": plane, "in": 3 * plane // 2, "out": plane // 2}
    place_array = jnp.stack([place["z"], place["y"], place["x"]]).astype(jnp.int32)
    kept = [name for name in names if name in earlier]
    pieces = found[0] + found[1]

    def owner(step, at):
        return lax.rem(at[0] + (line - step), line)

    def at_layer(layer):
        return lambda step, at: (layer, 0, owner(step, at), 0, 0)

    done = pl.pallas_call(
        functools.partial(assemble_kernel, sizes, names, kinds),
        grid_spec=pltpu.PrefetchScalarGridSpec(
            num_scalar_prefetch=1,
            grid=(line,),
            in_specs=[pl.BlockSpec((None, *pieces[0].shape[1:]), lambda step, at: (step, 0, 0))] * len(pieces)
            + [pl.BlockSpec(memory_space=pl.ANY)] * len(kept),
            out_specs=[
                pl.BlockSpec((None, counts[name], None, *shapes[name]), at_layer(layers[name])) for name in names
            ],
        ),
        out_shape=[sds((2, counts[name], line, *shapes[name]), F32) for name in names],
        input_output_aliases={1 + len(pieces) + number: names.index(name) for number, name in enumerate(kept)},
        compiler_params=params(),
        cost_estimate=cost(0, pieces * 3),
        name="assemble_" + "_".join(names),
    )(place_array, *pieces, *[earlier[name] for name in kept])
    return {**earlier, **dict(zip(names, done))}


def layer_forward(layer, x, ends, own, other, small, gain, shift):
    query, key, value, probs, mixed, normed1, rate1 = attend_forward(layer, x, ends, own, other, small, shift)
    act, dg, result, normed2, rate2 = feed_forward(layer, normed1, own, other, small, gain, shift)
    return result, (query, key, value, probs, mixed), (normed2, rate2, normed1, rate1, act, dg)


def prepare_small(b_in, b_up, rel_table):
    layers, _, local = b_in.shape
    units = b_up.shape[1]
    heads, span = rel_table.shape[1:]
    steps = local // LANES
    tile = units // steps
    head_dim = local // heads
    flat = jnp.concatenate([b_in.astype(F32).reshape(-1), b_up.astype(F32).reshape(-1), rel_table.reshape(-1)])
    again = swap(flat)

    def parts(vector):
        cut = layers * 2 * local
        end = cut + layers * units
        return (
            vector[:cut].reshape(layers, 2, steps, LANES).transpose(0, 2, 1, 3),
            vector[cut:end].reshape(layers, units // tile, 1, tile),
            vector[end:].reshape(layers, steps, heads // steps, span),
        )

    own, other = parts(flat), parts(again)
    tables = jnp.concatenate([own[2], other[2]], axis=2)
    return {
        "head_dim": head_dim,
        "b_in": jnp.concatenate([own[0], other[0]], axis=3),
        "b_up": jnp.concatenate([own[1], other[1]], axis=3),
        "table": [jnp.pad(tables[0], ((0, 0), (0, 0), (span // 2, span // 2)), mode="edge"), tables[1]],
    }


def small_pack_kernel(head_ref, *refs):
    inputs, outs = refs[:-2], refs[-2:]
    head = head_ref[0]
    row = 0
    for layer in (0, 1):
        gb, gbu, table, norms = inputs[4 * layer : 4 * layer + 4]
        steps, span, local = gb.shape[0], outs_span(table, layer), norms.shape[1] // 2
        tile, heads = gbu.shape[2] // 2, table.shape[1] // 2
        extra = (table.shape[2] - span) // 2
        for slot in range(2):
            for step in range(steps):
                for side, out in enumerate(outs):
                    out[row : row + 1, :] = gb[step, slot : slot + 1, side * LANES : (side + 1) * LANES]
                row += 1
        for step in range(gbu.shape[0]):
            for at in range(0, tile, LANES):
                for side, out in enumerate(outs):
                    out[row : row + 1, :] = gbu[step, :, side * tile + at : side * tile + at + LANES]
                row += 1
        lane = lax.broadcasted_iota(jnp.int32, (1, LANES), 1)
        for step in range(steps):
            for number in range(heads):
                for side, out in enumerate(outs):
                    values = table[step, side * heads + number : side * heads + number + 1, :]
                    for at in range(0, span, LANES):
                        part = values[:, extra + at : extra + at + LANES]
                        if extra and at == 0:
                            part = part + jnp.where(lane == 0, jnp.sum(values[:, :extra], axis=1, keepdims=True), 0.0)
                        if extra and at == span - LANES:
                            rest = jnp.sum(values[:, extra + span :], axis=1, keepdims=True)
                            part = part + jnp.where(lane == LANES - 1, rest, 0.0)
                        out[row + at // LANES : row + at // LANES + 1, :] = part
                row += span // LANES
        for number in range(6):
            for at in range(0, local, LANES):
                low = norms[number : number + 1, at : at + LANES]
                high = norms[number : number + 1, local + at : local + at + LANES]
                outs[0][row : row + 1, :] = jnp.where(head == 0, low, high)
                outs[1][row : row + 1, :] = jnp.where(head == 0, high, low)
                row += 1


def outs_span(table, layer):
    return table.shape[2] // 2 if layer == 0 else table.shape[2]


def small_pack(layers, head):
    flat = [array for grads in layers for array in grads]
    gb, gbu, table, norms = layers[1]
    half = gb.size // 2 + gbu.size // 2 + table.size // 2 + 6 * norms.shape[1] // 2
    shape = sds((2 * half // LANES, LANES), F32)
    return pl.pallas_call(
        small_pack_kernel,
        in_specs=[pl.BlockSpec(memory_space=pltpu.SMEM)] + [pl.BlockSpec(memory_space=pltpu.VMEM)] * len(flat),
        out_specs=[pl.BlockSpec(memory_space=pltpu.VMEM)] * 2,
        out_shape=[shape, shape],
        cost_estimate=cost(0, flat * 2),
        name="small_pack",
    )(head.astype(jnp.int32).reshape(1), *flat)


def small_unpack_kernel(total_ref, b_in, b_up, rel, gain, shift):
    row = 0
    for layer in (0, 1):
        for rows, out in ((b_in.shape[1], b_in), (1, b_up), (rel.shape[1], rel), (2, gain), (4, shift)):
            for number in range(rows):
                for at in range(0, out.shape[2], LANES):
                    out[layer, number : number + 1, at : at + LANES] = total_ref[row : row + 1, :]
                    row += 1


def small_unpack(total, b_in, b_up, rel, width):
    shapes = [b_in, (b_up[0], 1, b_up[1]), rel, (2, 2, width), (2, 4, width)]
    out = pl.pallas_call(
        small_unpack_kernel,
        out_shape=[sds(shape, F32) for shape in shapes],
        cost_estimate=cost(0, [total, total]),
        name="small_unpack",
    )(total)
    return out[0], out[1].reshape(b_up), out[2], out[3], out[4]


def per_device(
    tokens, lengths, w_in, b_in, w_out, w_up, b_up, w_down, norm_gain, norm_bias, rel_table, d_pooled, d_skip
):
    devices = lax.axis_size("dev") * lax.axis_size("head")
    count, piece, width = tokens.shape
    pooled_piece = piece // 2
    rows = -(-count // devices)
    padded = rows * devices
    extra = padded - count
    span = rel_table.shape[2]
    head = lax.axis_index("head")
    index = head * lax.axis_size("dev") + lax.axis_index("dev")
    both = ("head", "dev")
    norm_cols = width // lax.axis_size("head")

    def to_rows(array):
        array = jnp.pad(array, ((0, extra), (0, 0), (0, 0)))
        return lax.all_to_all(array, both, split_axis=0, concat_axis=1, tiled=True)

    def to_places(array):
        return lax.all_to_all(array, both, split_axis=1, concat_axis=0, tiled=True)[:count]

    sizes = grid_sizes(lax.axis_size("dev"))
    place = place_of(lax.axis_index("dev"), sizes)
    x0 = to_rows(tokens)
    own = {"w_in": w_in, "w_out": w_out, "w_up": w_up, "w_down": w_down}
    other = {name: swap(array) for name, array in own.items()}
    small = prepare_small(b_in, b_up, rel_table)
    second_grad = plain_call(
        pair_sum_kernel,
        sds((count * pooled_piece, width), BF),
        d_skip.reshape(count * piece, width),
        d_pooled.reshape(count * pooled_piece, width),
    ).reshape(count, pooled_piece, width)
    x0, second_grad = lax.optimization_barrier((x0, second_grad))
    grad_rows = to_rows(second_grad)
    ends = lax.dynamic_slice_in_dim(jnp.pad(jnp.cumsum(lengths, axis=1), ((0, extra), (0, 0))), index * rows, rows, 0)

    first, keep_a0, keep_f0 = layer_forward(0, x0, ends, own, other, small, norm_gain[0], norm_bias[0])
    pooled = span // 2
    x1 = first.reshape(rows, pooled, width)
    second, keep_a1, keep_f1 = layer_forward(1, x1, ends, own, other, small, norm_gain[1], norm_bias[1])
    pooled_out = to_places(second.reshape(rows, pooled, width))

    def feed_reductions(up, down):
        return [Reduction(up, sizes, place, ORDERS[0]), Reduction(down, sizes, place, ORDERS[1])]

    def attend_reductions(array):
        return [Reduction(array, sizes, place, order, half, 2) for half, order in enumerate(ORDERS)]

    def moves(group, level, sends):
        return [each.moves(level, arrays) for each, arrays in zip(group, sends)]

    def first_sends(group, arrays):
        for each, array in zip(group, arrays):
            each.absorb(array)
        return [each.first_sends() for each in group]

    def second_sends(group, received):
        for each, arrays in zip(group, received):
            each.first = arrays
        return [each.second_sends() for each in group]

    def settle_second(group, received):
        for each, arrays in zip(group, received):
            each.second = arrays

    grad = grad_rows.reshape(rows * pooled, width)
    outs = feed_backward(1, grad, keep_f1, own, other, small, norm_gain[1], norm_bias[1])
    outs, pooled_out = tie(outs, pooled_out)
    gwu_a, gwu_b, gwd_a, gwd_b, gbu1, grad_att, grad_resid, norms1 = outs
    feed1 = feed_reductions(gwu_a, gwd_a)
    sends_f1 = first_sends(feed1, [swap(gwu_b), swap(gwd_b)])
    outs = attend_backward(
        1, grad_att, grad_resid, x1, keep_a1, own, other, small, after=jax.tree.leaves(sends_f1)
    )
    outs, got_f1 = tie(outs, moves(feed1, 0, sends_f1))
    g_a, g_b, gb1, table1, grad = outs
    att1 = attend_reductions(g_a)
    g_b = swap(g_b)
    sends_f1, sends_a1 = second_sends(feed1, got_f1), first_sends(att1, [g_b, g_b])
    outs = feed_backward(
        0, grad, keep_f0, own, other, small, norm_gain[0], norm_bias[0], after=jax.tree.leaves((sends_a1, sends_f1))
    )
    outs, got_a1, got_f1 = tie(outs, moves(att1, 0, sends_a1), moves(feed1, 1, sends_f1))
    gwu_a, gwu_b, gwd_a, gwd_b, gbu0, grad_att, grad_resid, norms0 = outs
    feed0 = feed_reductions(gwu_a, gwd_a)
    settle_second(feed1, got_f1)
    packed1, sends_a1 = pack(feed1, place), second_sends(att1, got_a1)
    sends_f0 = first_sends(feed0, [swap(gwu_b), swap(gwd_b)])
    outs = attend_backward(
        0, grad_att, grad_resid, x0, keep_a0, own, other, small,
        after=jax.tree.leaves((sends_f0, sends_a1, packed1)),
        places=devices if piece % 16 == 0 else 0,
    )
    outs, got_f0, got_a1, pieces1 = tie(
        outs, moves(feed0, 0, sends_f0), moves(att1, 1, sends_a1), along_z(packed1, sizes)
    )
    g_a, g_b, gb0, table0, grad = outs
    att0 = attend_reductions(g_a)
    settle_second(att1, got_a1)
    line1 = line_of(line_sum(pieces1), sizes)
    g_b = swap(g_b)
    sends_f0, sends_a0 = second_sends(feed0, got_f0), first_sends(att0, [g_b, g_b])
    got_a0, got_f0, line1 = tie(moves(att0, 0, sends_a0), moves(feed0, 1, sends_f0), line1)
    settle_second(feed0, got_f0)
    mine, theirs = small_pack(((gb0, gbu0, table0, norms0), (gb1, gbu1, table1, norms1)), head)
    packed10 = pack([att1[0], feed0[0], att1[1], feed0[1]], place)
    sends_a0 = second_sends(att0, got_a0)
    pieces10, got_a0, plane1, theirs = tie(
        along_z(packed10, sizes), moves(att0, 1, sends_a0), plane_of(line1, sizes), swap(theirs)
    )
    settle_second(att0, got_a0)
    line10, pieces0, found1, grad, total_small = tie(
        line_of(line_sum(pieces10), sizes),
        along_z(pack(att0, place), sizes),
        all_of(plane1, sizes),
        grad,
        pair_sum(mine + theirs, sizes, "x", 1),
    )
    total_small = pair_sum_rest(total_small, sizes, "x")
    plane10, line0, total_small, grad = tie(
        plane_of(line10, sizes), line_of(line_sum(pieces0), sizes), pair_sum(total_small, sizes, "y", 1), grad
    )
    total_small = pair_sum_rest(total_small, sizes, "y")
    whole_tiles = on_tiles(feed1 + att1)
    block = {
        "up": (feed1[0].rows, feed1[0].cols),
        "down": (feed1[1].rows, feed1[1].cols),
        "in": (att1[0].rows, att1[0].cols),
        "out": (att1[0].rows, att1[0].cols),
    }
    found10, total_small, grad = tie(all_of(plane10, sizes), pair_sum(total_small, sizes, "z", 1), grad)
    if piece % 16 == 0:
        grad_in = lax.all_to_all(grad, both, split_axis=0, concat_axis=0, tiled=True)
        grad_in = grad_in.reshape(padded, piece, width)[:count]
    else:
        grad_in = to_places(grad.reshape(rows, span, width))
    sums = {}
    if whole_tiles:
        sums = assemble(found1, (("up",), ("down",)), {"up": 1, "down": 1}, block, sizes, place, sums)
    plane0, sums = tie(plane_of(line0, sizes), sums)
    if whole_tiles:
        layers = {"up": 0, "down": 0, "in": 1, "out": 1}
        sums = assemble(found10, (("low", "up"), ("high", "down")), layers, block, sizes, place, sums)
    total_small = pair_sum_rest(total_small, sizes, "z")
    found0, total_small, sums = tie(all_of(plane0, sizes), total_small, sums)
    flat_tokens = tokens.reshape(count * piece, width)
    skips = plain_call(
        skip_kernel,
        (sds(flat_tokens.shape, BF), sds(flat_tokens.shape, BF)),
        flat_tokens,
        d_skip.reshape(count * piece, width),
        pooled_out.reshape(count * pooled_piece, width),
        grad_in.reshape(count * piece, width),
    )
    skip_sum, d_input = skips
    g_b_in, g_b_up, g_rel, g_gain, g_bias = small_unpack(
        total_small, b_in.shape, b_up.shape, rel_table.shape, norm_cols
    )

    if whole_tiles:
        sums = assemble(found0, (("low",), ("high",)), {"in": 0, "out": 0}, block, sizes, place, sums)
        g_w_up, g_w_down, g_w_in, g_w_out = [sums[name] for name in ("up", "down", "in", "out")]
    else:
        gathered = [lax.all_gather(line[0], "dev", axis=0, tiled=False) for line in (line1, line10, line0)]
        g_w_up, g_w_down, g_w_in, g_w_out = assemble_small(
            *gathered, feed1, att1, feed0, att0, sizes
        )

    return (
        pooled_out,
        skip_sum.reshape(tokens.shape),
        d_input.reshape(tokens.shape),
        g_w_in.reshape(w_in.shape),
        g_b_in,
        g_w_out.reshape(2, width, w_in.shape[3]).transpose(0, 2, 1),
        g_w_up.reshape(w_up.shape),
        g_b_up,
        g_w_down.reshape(w_down.shape),
        g_gain,
        g_bias,
        g_rel,
    )


def solution(mesh):
    in_specs = (
        P(None, ("head", "dev"), None),
        P(),
        P(None, None, None, "head"),
        P(None, None, "head"),
        P(None, "head", None),
        P(None, None, "head"),
        P(None, "head"),
        P(None, "head", None),
        P(),
        P(),
        P(None, "head", None),
        P(None, ("head", "dev"), None),
        P(None, ("head", "dev"), None),
    )
    out_specs = (
        P(None, ("head", "dev"), None),
        P(None, ("head", "dev"), None),
        P(None, ("head", "dev"), None),
        P(None, None, None, "head"),
        P(None, None, "head"),
        P(None, "head", None),
        P(None, None, "head"),
        P(None, "head"),
        P(None, "head", None),
        P(None, None, "head"),
        P(None, None, "head"),
        P(None, "head", None),
    )
    return jax.shard_map(per_device, mesh=mesh, in_specs=in_specs, out_specs=out_specs, check_vma=False)
```

```python
import functools

import jax
import jax.numpy as jnp
from jax import lax
from jax.experimental import pallas as pl
from jax.experimental.pallas import tpu as pltpu
from jax.sharding import PartitionSpec as P

EPS = 1e-06
LANES = 128
BF = jnp.bfloat16
F32 = jnp.float32
VMEM_LIMIT = 56 * 1024 * 1024
ORDERS = ("xy", "yx")
ROW_BLOCK = 32


def dot(left, right):
    return lax.dot_general(left, right, (((1,), (0,)), ((), ())), preferred_element_type=F32)


def dot_nt(left, right):
    return lax.dot_general(left, right, (((1,), (1,)), ((), ())), preferred_element_type=F32)


def dot_tn(left, right):
    return lax.dot_general(left, right, (((0,), (0,)), ((), ())), preferred_element_type=F32)


def pool_matrix(count):
    place = lax.broadcasted_iota(jnp.int32, (count // 2, count), 0)
    token = lax.broadcasted_iota(jnp.int32, (count // 2, count), 1)
    return jnp.where((token >> 1) == place, 0.5, 0.0).astype(BF)


def spread_matrix(count):
    place = lax.broadcasted_iota(jnp.int32, (count, count // 2), 1)
    token = lax.broadcasted_iota(jnp.int32, (count, count // 2), 0)
    return jnp.where((token >> 1) == place, 0.5, 0.0).astype(BF)


def head_mask(width, head_dim, head, value):
    lane = lax.broadcasted_iota(jnp.int32, (1, width), 1)
    return jnp.where(lane // head_dim == head, value, 0.0).astype(BF)


def blocks(count, size):
    return [slice(at, at + size) for at in range(0, count, size)]


def norm_forward(total, n_out, rate_out):
    for here in blocks(n_out.shape[0], ROW_BLOCK):
        values = total(here)
        center = values - jnp.mean(values, axis=-1, keepdims=True)
        spread = jnp.mean(center * center, axis=-1, keepdims=True)
        rate = lax.rsqrt(spread + EPS)
        n_out[here, :] = center * rate
        rate_out[here, :] = jnp.broadcast_to(rate, (ROW_BLOCK, rate_out.shape[1]))


def norm_backward(grad, normed, rates, gain, put):
    sums = [jnp.zeros((1, normed.shape[1]), F32) for _ in range(3)]
    for here in blocks(normed.shape[0], ROW_BLOCK):
        values, unit = grad[here, :].astype(F32), normed[here, :]
        scaled = values * gain
        mean_one = jnp.mean(scaled, axis=-1, keepdims=True)
        mean_two = jnp.mean(scaled * unit, axis=-1, keepdims=True)
        back = (scaled - mean_one - unit * mean_two) * rates[here, 0:1]
        put(here, back)
        for number, part in enumerate((values * unit, values, back)):
            sums[number] = sums[number] + jnp.sum(part, axis=0, keepdims=True)
    return sums


def row_documents(ends_ref, row, count_q, count_k, step_q, step_k):
    at_q = lax.broadcasted_iota(jnp.int32, (count_q, 1), 0) * step_q
    at_k = lax.broadcasted_iota(jnp.int32, (1, count_k), 1) * step_k
    doc_q = jnp.zeros((count_q, 1), jnp.int32)
    doc_k = jnp.zeros((1, count_k), jnp.int32)
    for number in range(ends_ref.shape[1]):
        end = ends_ref[row, number]
        doc_q = doc_q + (at_q >= end).astype(jnp.int32)
        doc_k = doc_k + (at_k >= end).astype(jnp.int32)
    return doc_q, doc_k


def fill_bias(bias_ref, head, table_row, stride):
    count_q, count_k = bias_ref.shape[1:]
    span = table_row.shape[1]
    base = jnp.concatenate([pltpu.roll(table_row, stride * low, 1) for low in range(8)], axis=0)
    step = 8 * stride
    for turn in range(LANES // step):
        back = (span // 2 - step * turn) % LANES
        rolled = pltpu.roll(base, (span - back) % span, 1)
        for block in range(turn, count_q // 8, LANES // step):
            at = span // 2 - step * block - back
            bias_ref[head, 8 * block : 8 * block + 8, :] = rolled[:, at : at + count_k]


def unroll_sum(block_values, count_q, count_k, span, stride):
    total = jnp.zeros((8, span), F32)
    step = 8 * stride
    for turn in range(LANES // step):
        back = (span // 2 - step * turn) % LANES
        part = jnp.zeros((8, span), F32)
        for block in range(turn, count_q // 8, LANES // step):
            at = span // 2 - step * block - back
            columns = [block_values(block)]
            if at:
                columns = [jnp.zeros((8, at), F32)] + columns
            if span - at - count_k:
                columns = columns + [jnp.zeros((8, span - at - count_k), F32)]
            part = part + jnp.concatenate(columns, axis=1)
        total = total + pltpu.roll(part, back, 1)
    out = total[0:1]
    for low in range(1, 8):
        out = out + pltpu.roll(total[low : low + 1], (span - stride * low) % span, 1)
    return out


def with_extras(kernel, count):
    def run(*refs, inputs):
        return kernel(*refs[:inputs], *refs[inputs + count :])

    return run


def call(kernel, in_specs, operands, after=(), **kwargs):
    if after:
        body = functools.partial(with_extras(kernel, len(after)), inputs=len(operands))
        in_specs = list(in_specs) + [pl.BlockSpec(memory_space=pl.ANY)] * len(after)
    else:
        body = kernel
    return pl.pallas_call(body, in_specs=in_specs, **kwargs)(*operands, *after)


def attend_forward_kernel(
    pooling, rows, heads, head_dim,
    ends_ref, x_ref, wi_a, wi_b, bias_in_ref, wo_a, wo_b, tab_ref, shift_ref,
    q_out, k_out, v_out, p_out, mix_out, n_out, rate_out,
    acc_ref, bias_ref, query_ref, score_ref, *resid_ref,
):
    step = pl.program_id(0)
    last = pl.num_programs(0) - 1
    count_k = x_ref.shape[1]
    count_q = acc_ref.shape[0] // rows
    width = x_ref.shape[2]
    group = heads * head_dim
    stride = 2 if pooling else 1

    @pl.when(step == 0)
    def _():
        if pooling:
            pool = pool_matrix(count_k)
            for row in range(rows):
                pooled = dot(pool, x_ref[row])
                resid_ref[0][row * count_q : (row + 1) * count_q, :] = pooled
                query_ref[row * count_q : (row + 1) * count_q, :] = pooled.astype(BF)
        else:
            query_ref[...] = x_ref[...].reshape(rows * count_q, width)
        acc_ref[...] = jnp.zeros_like(acc_ref)

    x = x_ref[...].reshape(rows * count_k, width)
    wq = jnp.concatenate([wi_a[0], wi_b[0]], axis=1)
    wk = jnp.concatenate([wi_a[1], wi_b[1]], axis=1)
    wv = jnp.concatenate([wi_a[2], wi_b[2]], axis=1)
    query = (dot(query_ref[...], wq) + bias_in_ref[0:1, :]).astype(BF)
    key = dot(x, wk).astype(BF)
    value = (dot(x, wv) + bias_in_ref[1:2, :]).astype(BF)
    q_out[...] = query
    k_out[...] = key
    v_out[...] = value
    for head in range(heads):
        fill_bias(bias_ref, head, tab_ref[head : head + 1, :], stride)
    lane = lax.broadcasted_iota(jnp.int32, (1, group), 1) // head_dim
    for row in range(rows):
        q_row = query[row * count_q : (row + 1) * count_q]
        masked = [q_row * head_mask(group, head_dim, head, head_dim ** (-0.5)) for head in range(heads)]
        score_ref[row] = dot_nt(jnp.concatenate(masked, axis=0), key[row * count_k : (row + 1) * count_k])
    for row in range(rows):
        doc_q, doc_k = row_documents(ends_ref, row, count_q, count_k, 2, 2 // stride)
        for head in range(heads):
            for here in blocks(count_q, ROW_BLOCK):
                at = slice(head * count_q + here.start, head * count_q + here.stop)
                same = doc_q[here] == doc_k
                scores = jnp.where(same, score_ref[row, at, :] + bias_ref[head, here, :], -1e30)
                top = jnp.max(scores, axis=-1, keepdims=True)
                expo = jnp.exp(scores - top)
                denom = jnp.sum(expo, axis=-1, keepdims=True)
                p_out[row, at, :] = (expo * (1.0 / denom)).astype(BF)
    for row in range(rows):
        every = dot(p_out[row], value[row * count_k : (row + 1) * count_k])
        mixed = every[:count_q]
        for head in range(1, heads):
            mixed = jnp.where(lane == head, every[head * count_q : (head + 1) * count_q], mixed)
        mix_out[row * count_q : (row + 1) * count_q, :] = mixed.astype(BF)
    wo = jnp.concatenate([wo_a[...], wo_b[...]], axis=0)
    acc_ref[...] += dot(mix_out[...], wo)

    @pl.when(step == last)
    def _():

        def total_of(here):
            resid = resid_ref[0][here, :] if pooling else query_ref[here, :].astype(F32)
            return acc_ref[here, :] + shift_ref[0:1, :] + resid

        norm_forward(total_of, n_out, rate_out)


def feed_forward_kernel(
    n_ref, gain_ref, shift_ref, wu_a, wu_b, bu_ref, wd_a, wd_b,
    act_out, dg_out, res_out, n_out, rate_out,
    mid_ref, acc_ref, up_ref,
):
    step = pl.program_id(0)
    last = pl.num_programs(0) - 1
    tile = wu_a.shape[1]

    @pl.when(step == 0)
    def _():
        middle = n_ref[...] * gain_ref[0:1, :] + shift_ref[1:2, :]
        mid_ref[...] = middle.astype(BF)
        acc_ref[...] = middle + shift_ref[2:3, :]

    for number, wu in enumerate((wu_a, wu_b)):
        up_ref[number] = dot(mid_ref[...], wu[...])
    for number in range(2):
        cols = slice(number * tile, (number + 1) * tile)
        for here in blocks(up_ref.shape[1], ROW_BLOCK):
            up = up_ref[number, here, :] + bu_ref[:, cols]
            cdf = 0.5 * (1.0 + lax.erf(up * (0.5**0.5)))
            density = jnp.exp(up * up * (-0.5)) * 0.3989422804014327
            dg_out[here, cols] = (cdf + up * density).astype(BF)
            act_out[here, cols] = (up * cdf).astype(BF)
    acc_ref[...] += dot(act_out[:, :tile], wd_a[...]) + dot(act_out[:, tile:], wd_b[...])

    @pl.when(step == last)
    def _():
        norm_forward(lambda here: acc_ref[here, :], n_out, rate_out)
        res_out[...] = (n_out[...] * gain_ref[1:2, :] + shift_ref[3:4, :]).astype(BF)


def feed_backward_kernel(
    grad_ref, n2_ref, rate2_ref, n1_ref, rate1_ref, gain_ref, shift_ref, act_ref, dg_ref, wu_a, wu_b, wd_a, wd_b,
    gwu_a, gwu_b, gwd_a, gwd_b, gbu_out, att_out, resid_out, small_out,
    down_ref, mid_t_ref, acc_ref, up_ref,
):
    step = pl.program_id(0)
    last = pl.num_programs(0) - 1
    tile = wu_a.shape[1]

    @pl.when(step == 0)
    def _():

        def put(here, back):
            down_ref[here, :] = back.astype(BF)
            acc_ref[here, :] = back

        row_gain, row_shift, row_out = norm_backward(grad_ref, n2_ref, rate2_ref, gain_ref[1:2, :], put)
        small_out[...] = jnp.zeros_like(small_out)
        small_out[1:2, :] = row_gain
        small_out[4:5, :] = row_out
        small_out[5:6, :] = row_shift
        middle = (n1_ref[...] * gain_ref[0:1, :] + shift_ref[1:2, :]).astype(BF)
        mid_t_ref[...] = middle.T

    for number, (wd, gwd) in enumerate(((wd_a, gwd_a), (wd_b, gwd_b))):
        cols = slice(number * tile, (number + 1) * tile)
        grad_act = dot_nt(down_ref[...], wd[...])
        gwd[...] = dot_tn(act_ref[:, cols], down_ref[...]).astype(BF)
        summed = jnp.zeros((1, tile), F32)
        for here in blocks(grad_act.shape[0], ROW_BLOCK):
            grad_up = (grad_act[here] * dg_ref[here, cols].astype(F32)).astype(BF)
            up_ref[here, cols] = grad_up
            summed = summed + jnp.sum(grad_up.astype(F32), axis=0, keepdims=True)
        gbu_out[:, cols] = summed
    gwu_a[...] = dot(mid_t_ref[...], up_ref[:, :tile]).astype(BF)
    gwu_b[...] = dot(mid_t_ref[...], up_ref[:, tile:]).astype(BF)
    acc_ref[...] += dot_nt(up_ref[:, :tile], wu_a[...]) + dot_nt(up_ref[:, tile:], wu_b[...])

    @pl.when(step == last)
    def _():

        def put(here, back):
            att_out[here, :] = back.astype(BF)
            resid_out[here, :] = back

        row_gain, row_shift, row_out = norm_backward(acc_ref, n1_ref, rate1_ref, gain_ref[0:1, :], put)
        small_out[0:1, :] = row_gain
        small_out[2:3, :] = row_out
        small_out[3:4, :] = row_shift


def attend_backward_kernel(
    pooling, rows, heads, head_dim,
    att_ref, resid_ref, x_ref, q_ref, k_ref, v_ref, p_ref, mix_ref, wi_a, wi_b, wo_a, wo_b,
    g_a, g_b, gb_out, tab_out, in_out,
    x_t_ref, query_t_ref, att_t_ref, acc_k_ref, acc_q_ref, ds_ref, dp_ref, dom_ref, qm_ref, dq_ref, dkv_ref,
):
    step = pl.program_id(0)
    last = pl.num_programs(0) - 1
    count_k = x_ref.shape[1]
    count_q = att_ref.shape[0] // rows
    width = x_ref.shape[2]
    group = heads * head_dim
    stride = 2 if pooling else 1
    span = tab_out.shape[1]

    @pl.when(step == 0)
    def _():
        x = x_ref[...].reshape(rows * count_k, width)
        x_t_ref[...] = x.T
        if pooling:
            pool = pool_matrix(count_k)
            for row in range(rows):
                query_t_ref[:, row * count_q : (row + 1) * count_q] = dot(pool, x_ref[row]).astype(BF).T
        att_t_ref[...] = att_ref[...].T
        if pooling:
            acc_k_ref[...] = jnp.zeros_like(acc_k_ref)
            acc_q_ref[...] = resid_ref[...]
        else:
            acc_k_ref[...] = resid_ref[...]

    wo = jnp.concatenate([wo_a[...], wo_b[...]], axis=0)
    grad_mixed = dot_nt(att_ref[...], wo).astype(BF)
    lane = lax.broadcasted_iota(jnp.int32, (1, group), 1) // head_dim
    for row in range(rows):
        q_row = q_ref[row * count_q : (row + 1) * count_q, :]
        g_row = grad_mixed[row * count_q : (row + 1) * count_q]
        for head in range(heads):
            at = slice(head * count_q, (head + 1) * count_q)
            dom_ref[row, at, :] = g_row * head_mask(group, head_dim, head, 1.0)
            qm_ref[row, at, :] = q_row * head_mask(group, head_dim, head, head_dim ** (-0.5))
        dp_ref[row] = dot_nt(dom_ref[row], v_ref[row * count_k : (row + 1) * count_k, :])
    for row in range(rows):
        for at in blocks(heads * count_q, ROW_BLOCK):
            probs = p_ref[row, at, :].astype(F32)
            terms = probs * dp_ref[row, at, :]
            ds_ref[row, at, :] = (terms - probs * jnp.sum(terms, axis=-1, keepdims=True)).astype(BF)
    for row in range(rows):
        keys = slice(row * count_k, (row + 1) * count_k)
        every = dot(ds_ref[row], k_ref[keys, :])
        grad_q = every[:count_q]
        for head in range(1, heads):
            grad_q = jnp.where(lane == head, every[head * count_q : (head + 1) * count_q], grad_q)
        dq_ref[row * count_q : (row + 1) * count_q, :] = (grad_q * head_dim ** (-0.5)).astype(BF)
        dkv_ref[keys, :group] = dot_tn(ds_ref[row], qm_ref[row]).astype(BF)
        dkv_ref[keys, group:] = dot_tn(p_ref[row], dom_ref[row]).astype(BF)
    for head in range(heads):


        def block_values(block, first=head * count_q):
            at = slice(first + 8 * block, first + 8 * block + 8)
            return functools.reduce(jnp.add, [ds_ref[row, at, :].astype(F32) for row in range(rows)])

        tab_out[head : head + 1, :] = unroll_sum(block_values, count_q, count_k, span, stride)
    half = group // 2
    query_t = query_t_ref[...] if pooling else x_t_ref[...]
    grad_wq = dot(query_t, dq_ref[...]).astype(BF)
    grad_wk = dot(x_t_ref[...], dkv_ref[:, :group]).astype(BF)
    grad_wv = dot(x_t_ref[...], dkv_ref[:, group:]).astype(BF)
    grad_wo = dot(att_t_ref[...], mix_ref[...]).astype(BF)
    for slot, grad in enumerate((grad_wq, grad_wk, grad_wv, grad_wo)):
        g_a[slot] = grad[:, :half]
        g_b[slot] = grad[:, half:]
    gb_out[0:1, :] = jnp.sum(dq_ref[...].astype(F32), axis=0, keepdims=True)
    gb_out[1:2, :] = jnp.sum(dkv_ref[:, group:].astype(F32), axis=0, keepdims=True)
    wq = jnp.concatenate([wi_a[0], wi_b[0]], axis=1)
    wkv = jnp.concatenate([wi_a[1], wi_b[1], wi_a[2], wi_b[2]], axis=1)
    if pooling:
        acc_q_ref[...] += dot_nt(dq_ref[...], wq)
        acc_k_ref[...] += dot_nt(dkv_ref[...], wkv)
    else:
        acc_k_ref[...] += dot_nt(dq_ref[...], wq) + dot_nt(dkv_ref[...], wkv)

    @pl.when(step == last)
    def _():
        if pooling:
            spread = spread_matrix(count_k)
            for row in range(rows):
                total = acc_q_ref[row * count_q : (row + 1) * count_q, :]
                high = total.astype(BF)
                rest = (total - high.astype(F32)).astype(BF)
                keys = slice(row * count_k, (row + 1) * count_k)
                back = (acc_k_ref[keys, :] + dot(spread, high) + dot(spread, rest)).astype(BF)
                if len(in_out.shape) == 2:
                    in_out[keys, :] = back
                else:
                    in_out[:, row] = back.reshape(in_out.shape[0], *in_out.shape[2:])
        else:
            in_out[...] = acc_k_ref[...].astype(BF)


def whole(shape):
    return pl.BlockSpec(shape, lambda step: (0,) * len(shape))


def params():
    return pltpu.CompilerParams(dimension_semantics=("arbitrary",), vmem_limit_bytes=VMEM_LIMIT)


def cost(flops, arrays, transcendentals=0):
    moved = sum(array.size * array.dtype.itemsize for array in arrays)
    return pl.CostEstimate(flops=int(flops), bytes_accessed=int(moved), transcendentals=int(transcendentals))


def sds(shape, dtype):
    return jax.ShapeDtypeStruct(shape, dtype)


def attend_forward(layer, x, ends, own, other, small, shift):
    rows, count_k, width = x.shape
    pooling = layer == 0
    count_q = count_k // 2 if pooling else count_k
    wi_a, wo_a, wi_b, wo_b = own["w_in"], own["w_out"], other["w_in"], other["w_out"]
    local = wi_a.shape[3]
    steps = local // LANES
    head_dim = small["head_dim"]
    heads = 2 * LANES // head_dim
    group = 2 * LANES
    flat_q, flat_k = rows * count_q, rows * count_k
    table = small["table"][layer]
    span = table.shape[2]
    weight = pl.BlockSpec((None, 3, width, LANES), lambda step: (layer, 0, 0, step))
    out_w = pl.BlockSpec((None, LANES, width), lambda step: (layer, step, 0))
    out_shape = (
        sds((steps, flat_q, group), BF),
        sds((steps, flat_k, group), BF),
        sds((steps, flat_k, group), BF),
        sds((steps, rows, heads * count_q, count_k), BF),
        sds((steps, flat_q, group), BF),
        sds((flat_q, width), F32),
        sds((flat_q, LANES), F32),
    )
    scratch = [
        pltpu.VMEM((flat_q, width), F32),
        pltpu.VMEM((heads, count_q, count_k), F32),
        pltpu.VMEM((flat_q, width), BF),
        pltpu.VMEM((rows, heads * count_q, count_k), F32),
    ]
    if pooling:
        scratch.append(pltpu.VMEM((flat_q, width), F32))
    macs = (2 * flat_q + 2 * flat_k) * width * width + 2 * steps * group * flat_q * count_k * heads
    return pl.pallas_call(
        functools.partial(attend_forward_kernel, pooling, rows, heads, head_dim),
        grid=(steps,),
        in_specs=[
            pl.BlockSpec(memory_space=pltpu.SMEM),
            whole((rows, count_k, width)),
            weight,
            weight,
            pl.BlockSpec((None, 2, group), lambda step: (step, 0, 0)),
            out_w,
            out_w,
            pl.BlockSpec((None, heads, span), lambda step: (step, 0, 0)),
            whole(shift.shape),
        ],
        out_specs=[
            pl.BlockSpec((None, flat_q, group), lambda step: (step, 0, 0)),
            pl.BlockSpec((None, flat_k, group), lambda step: (step, 0, 0)),
            pl.BlockSpec((None, flat_k, group), lambda step: (step, 0, 0)),
            pl.BlockSpec((None, rows, heads * count_q, count_k), lambda step: (step, 0, 0, 0)),
            pl.BlockSpec((None, flat_q, group), lambda step: (step, 0, 0)),
            whole((flat_q, width)),
            whole((flat_q, LANES)),
        ],
        out_shape=out_shape,
        scratch_shapes=scratch,
        compiler_params=params(),
        cost_estimate=cost(2 * macs, out_shape, steps * heads * flat_q * count_k),
        name=f"attend_forward_{layer}",
    )(ends, x, wi_a, wi_b, small["b_in"][layer], wo_a, wo_b, table, shift)


def feed_forward(layer, normed, own, other, small, gain, shift):
    flat, width = normed.shape
    wu_a, wd_a, wu_b, wd_b = own["w_up"], own["w_down"], other["w_up"], other["w_down"]
    bias = small["b_up"][layer]
    steps, _, both = bias.shape
    tile = both // 2
    up_w = pl.BlockSpec((None, width, tile), lambda step: (layer, 0, step))
    down_w = pl.BlockSpec((None, tile, width), lambda step: (layer, step, 0))
    wide = pl.BlockSpec((None, flat, both), lambda step: (step, 0, 0))
    out_shape = (
        sds((steps, flat, both), BF),
        sds((steps, flat, both), BF),
        sds((flat, width), BF),
        sds((flat, width), F32),
        sds((flat, LANES), F32),
    )
    return pl.pallas_call(
        feed_forward_kernel,
        grid=(steps,),
        in_specs=[
            whole((flat, width)),
            whole(gain.shape),
            whole(shift.shape),
            up_w,
            up_w,
            pl.BlockSpec((None, 1, both), lambda step: (step, 0, 0)),
            down_w,
            down_w,
        ],
        out_specs=[wide, wide, whole((flat, width)), whole((flat, width)), whole((flat, LANES))],
        out_shape=out_shape,
        scratch_shapes=[
            pltpu.VMEM((flat, width), BF),
            pltpu.VMEM((flat, width), F32),
            pltpu.VMEM((2, flat, tile), F32),
        ],
        compiler_params=params(),
        cost_estimate=cost(4 * flat * width * steps * both, out_shape, 2 * flat * steps * both),
        name=f"feed_forward_{layer}",
    )(normed, gain, shift, wu_a, wu_b, bias, wd_a, wd_b)


def feed_backward(layer, grad, kept, own, other, small, gain, shift, after=()):
    normed2, rate2, normed1, rate1, act, dg = kept
    flat, width = normed1.shape
    wu_a, wd_a, wu_b, wd_b = own["w_up"], own["w_down"], other["w_up"], other["w_down"]
    steps, _, both = act.shape
    tile = both // 2
    units = steps * tile
    up_w = pl.BlockSpec((None, width, tile), lambda step: (layer, 0, step))
    down_w = pl.BlockSpec((None, tile, width), lambda step: (layer, step, 0))
    up_g = pl.BlockSpec((width, tile), lambda step: (0, step))
    down_g = pl.BlockSpec((tile, width), lambda step: (step, 0))
    wide = pl.BlockSpec((None, flat, both), lambda step: (step, 0, 0))
    out_shape = (
        sds((width, units), BF),
        sds((width, units), BF),
        sds((units, width), BF),
        sds((units, width), BF),
        sds((steps, 1, both), F32),
        sds((flat, width), BF),
        sds((flat, width), F32),
        sds((8, width), F32),
    )
    return call(
        feed_backward_kernel,
        grid=(steps,),
        operands=(grad, normed2, rate2, normed1, rate1, gain, shift, act, dg, wu_a, wu_b, wd_a, wd_b),
        after=after,
        in_specs=[
            whole((flat, width)),
            whole((flat, width)),
            whole((flat, LANES)),
            whole((flat, width)),
            whole((flat, LANES)),
            whole(gain.shape),
            whole(shift.shape),
            wide,
            wide,
            up_w,
            up_w,
            down_w,
            down_w,
        ],
        out_specs=[
            up_g,
            up_g,
            down_g,
            down_g,
            pl.BlockSpec((None, 1, both), lambda step: (step, 0, 0)),
            whole((flat, width)),
            whole((flat, width)),
            whole((8, width)),
        ],
        out_shape=out_shape,
        scratch_shapes=[
            pltpu.VMEM((flat, width), BF),
            pltpu.VMEM((width, flat), BF),
            pltpu.VMEM((flat, width), F32),
            pltpu.VMEM((flat, both), BF),
        ],
        compiler_params=params(),
        cost_estimate=cost(8 * flat * width * steps * both, out_shape + (act, dg)),
        name=f"feed_backward_{layer}",
    )


def attend_backward(layer, grad_att, grad_resid, x, kept, own, other, small, after=(), places=0):
    rows, count_k, width = x.shape
    pooling = layer == 0
    count_q = count_k // 2 if pooling else count_k
    query, key, value, probs, mixed = kept
    wi_a, wo_a, wi_b, wo_b = own["w_in"], own["w_out"], other["w_in"], other["w_out"]
    local = wi_a.shape[3]
    steps = local // LANES
    head_dim = small["head_dim"]
    heads = 2 * LANES // head_dim
    group = 2 * LANES
    flat_q, flat_k = rows * count_q, rows * count_k
    span = small["table"][layer].shape[2]
    weight = pl.BlockSpec((None, 3, width, LANES), lambda step: (layer, 0, 0, step))
    out_w = pl.BlockSpec((None, LANES, width), lambda step: (layer, step, 0))
    grad_w = pl.BlockSpec((4, width, LANES), lambda step: (0, 0, step))
    by_q = pl.BlockSpec((None, flat_q, group), lambda step: (step, 0, 0))
    by_k = pl.BlockSpec((None, flat_k, group), lambda step: (step, 0, 0))
    out_shape = (
        sds((4, width, local), BF),
        sds((4, width, local), BF),
        sds((steps, 2, group), F32),
        sds((steps, heads, span), F32),
        sds((places, rows, count_k // places, width) if places else (flat_k, width), BF),
    )
    macs = 2 * (2 * flat_q + 2 * flat_k) * width * width + 5 * steps * group * flat_q * count_k * heads
    return call(
        functools.partial(attend_backward_kernel, pooling, rows, heads, head_dim),
        grid=(steps,),
        operands=(grad_att, grad_resid, x, query, key, value, probs, mixed, wi_a, wi_b, wo_a, wo_b),
        after=after,
        in_specs=[
            whole((flat_q, width)),
            whole((flat_q, width)),
            whole((rows, count_k, width)),
            by_q,
            by_k,
            by_k,
            pl.BlockSpec((None, rows, heads * count_q, count_k), lambda step: (step, 0, 0, 0)),
            by_q,
            weight,
            weight,
            out_w,
            out_w,
        ],
        out_specs=[
            grad_w,
            grad_w,
            pl.BlockSpec((None, 2, group), lambda step: (step, 0, 0)),
            pl.BlockSpec((None, heads, span), lambda step: (step, 0, 0)),
            whole(out_shape[4].shape),
        ],
        out_shape=out_shape,
        scratch_shapes=[
            pltpu.VMEM((width, flat_k), BF),
            pltpu.VMEM((width, flat_q) if pooling else (8, LANES), BF),
            pltpu.VMEM((width, flat_q), BF),
            pltpu.VMEM((flat_k, width), F32),
            pltpu.VMEM((flat_q, width) if pooling else (8, LANES), F32),
            pltpu.VMEM((rows, heads * count_q, count_k), BF),
            pltpu.VMEM((rows, heads * count_q, count_k), F32),
            pltpu.VMEM((rows, heads * count_q, group), BF),
            pltpu.VMEM((rows, heads * count_q, group), BF),
            pltpu.VMEM((flat_q, group), BF),
            pltpu.VMEM((flat_k, 2 * group), BF),
        ],
        compiler_params=params(),
        cost_estimate=cost(2 * macs, out_shape + (probs,)),
        name=f"attend_backward_{layer}",
    )


def pair_sum_kernel(skip_ref, pooled_ref, out_ref):
    count = skip_ref.shape[0]
    part = 192
    pool = pool_matrix(part)
    for at in range(0, count, part):
        half = slice(at // 2, (at + part) // 2)
        pair = 2.0 * dot(pool, skip_ref[at : at + part, :])
        out_ref[half, :] = (pooled_ref[half, :].astype(F32) + pair).astype(BF)


def skip_kernel(tokens_ref, skip_ref, pooled_ref, grad_ref, sum_out, grad_out):
    count = tokens_ref.shape[0]
    part = 192
    spread = spread_matrix(part)
    for at in range(0, count, part):
        here = slice(at, at + part)
        again = 2.0 * dot(spread, pooled_ref[at // 2 : (at + part) // 2, :])
        sum_out[here, :] = (tokens_ref[here, :].astype(F32) + again).astype(BF)
        grad_out[here, :] = (skip_ref[here, :].astype(F32) + grad_ref[here, :].astype(F32)).astype(BF)


def plain_call(kernel, out_shape, *arrays):
    return pl.pallas_call(
        kernel,
        out_shape=out_shape,
        compiler_params=pltpu.CompilerParams(vmem_limit_bytes=VMEM_LIMIT),
        cost_estimate=cost(1e9, arrays),
    )(*arrays)


def swap(array):
    return lax.ppermute(array, "head", [(0, 1), (1, 0)])


def grid_sizes(devices):
    bits = devices.bit_length() - 1
    side = 1 << (bits // 3)
    return {"z": devices // (side * side), "y": side, "x": side}


def place_of(index, sizes):
    return {
        "z": index // (sizes["y"] * sizes["x"]),
        "y": (index // sizes["x"]) % sizes["y"],
        "x": index % sizes["x"],
    }


def moved(array, sizes, axis, target):
    count = sizes["z"] * sizes["y"] * sizes["x"]
    pairs = []
    for index in range(count):
        at = place_of(index, sizes)
        at[axis] = target(at[axis]) % sizes[axis]
        pairs.append((index, (at["z"] * sizes["y"] + at["y"]) * sizes["x"] + at["x"]))
    return lax.ppermute(array, "dev", pairs)


def shifted(array, sizes, axis, by):
    return moved(array, sizes, axis, lambda at: at + by)


def lines(sizes, axis):
    count = sizes["z"] * sizes["y"] * sizes["x"]
    found = {}
    for index in range(count):
        at = place_of(index, sizes)
        at[axis] = -1
        found.setdefault(tuple(at.values()), []).append(index)
    return list(found.values())


def pair_sum(array, sizes, axis, step):
    return array + moved(array, sizes, axis, lambda at: at ^ step)


def pair_sum_rest(array, sizes, axis):
    step = 2
    while step < sizes[axis]:
        array = pair_sum(array, sizes, axis, step)
        step *= 2
    return array


def pick(array, number):
    return lax.dynamic_index_in_dim(array, number, 0, keepdims=False)


def total(terms):
    return functools.reduce(jnp.add, [term.astype(F32) for term in terms]).astype(BF)


def tie(*groups):
    leaves, tree = jax.tree.flatten(groups)
    return jax.tree.unflatten(tree, lax.optimization_barrier(leaves))


class Reduction:
    def __init__(self, mine, sizes, place, order, half=0, halves=1):
        self.sizes, self.place, self.order = sizes, place, order + "z"
        self.size = [sizes[axis] for axis in self.order]
        cols = mine.shape[-1]
        rows = mine.size // cols // halves
        self.rows, self.cols = rows // (self.size[0] * self.size[1] * self.size[2]), cols
        self.shape = (halves * self.size[0], *self.size[1:], self.rows, cols)
        self.lead = half * self.size[0]
        self.base = [mine.reshape(self.shape)]
        self.first, self.second = [], []

    def absorb(self, array):
        self.base = self.base + [array.reshape(self.shape)]

    def first_sends(self):
        at, size = self.place[self.order[0]], self.size[0]
        return [total([pick(term, self.lead + (at + by) % size) for term in self.base]) for by in range(1, size)]

    def second_sends(self):
        at = self.lead + self.place[self.order[0]]
        here, size = self.place[self.order[1]], self.size[1]
        sends = []
        for by in range(1, size):
            to = (here + by) % size
            zero = jnp.zeros_like(to)
            corner = (at, to, zero, zero, zero)
            cut = (1, 1, *self.shape[2:])
            terms = [lax.dynamic_slice(term, corner, cut).reshape(self.shape[2:]) for term in self.base]
            sends.append(total(terms + [pick(term, to) for term in self.first]))
        return sends

    def moves(self, level, sends):
        return [shifted(array, self.sizes, self.order[level], by + 1) for by, array in enumerate(sends)]


def packed_rows(reduction):
    return -(-reduction.rows // 16) * 16


def pack_kernel(counts, place_ref, *refs):
    out_ref = refs[-1]
    width = out_ref.shape[1]
    start = at = 0
    for count in counts:
        terms = [ref[...].astype(F32) for ref in refs[start : start + count]]
        start += count
        summed = functools.reduce(jnp.add, terms).astype(BF)
        rows, cols = summed.shape
        for col in range(0, cols, width):
            out_ref[at : at + rows, :] = summed[:, col : col + width]
            at += -(-rows // 16) * 16


def on_tiles(reductions):
    return all(each.rows % 16 == 0 for each in reductions)


def pack_small(reductions, width):
    parts = []
    for each in reductions:
        at, here = each.lead + each.place[each.order[0]], each.place[each.order[1]]
        terms = [pick(pick(term, at), here) for term in each.base] + [pick(term, here) for term in each.first]
        summed = total(terms + each.second)
        for col in range(0, each.cols, width):
            part = summed[:, :, col : col + width]
            parts.append(jnp.pad(part, ((0, 0), (0, packed_rows(each) - each.rows), (0, 0))))
    return jnp.concatenate(parts, axis=1)


def unpack_small(gathered, reductions, sizes):
    width = gathered.shape[2]
    out, at = [], 0
    for each in reductions:
        parts = []
        for _ in range(0, each.cols, width):
            parts.append(gathered[:, at : at + each.rows])
            at += packed_rows(each)
        pieces = jnp.concatenate(parts, axis=2).reshape(
            *[sizes[axis] for axis in "zyx"], each.rows, each.cols
        )
        pieces = pieces.transpose(*["zyx".index(axis) for axis in each.order], 3, 4)
        out.append(pieces.reshape(-1, each.cols).astype(F32))
    return out


def assemble_small(gathered1, gathered10, gathered0, feed1, att1, feed0, att0, sizes):
    up1, down1 = unpack_small(gathered1, feed1, sizes)
    low1, up0, high1, down0 = unpack_small(gathered10, [att1[0], feed0[0], att1[1], feed0[1]], sizes)
    low0, high0 = unpack_small(gathered0, att0, sizes)
    half = high0.shape[0] // 2
    w_in = jnp.stack([jnp.concatenate([low0, high0[:half]]), jnp.concatenate([low1, high1[:half]])])
    w_out = jnp.stack([high0[half:], high1[half:]])
    return jnp.stack([up0, up1]), jnp.stack([down0, down1]), w_in, w_out


def pack(reductions, place):
    width = min(reduction.cols for reduction in reductions)
    line = reductions[0].size[2]
    operands, specs, counts = [], [], []
    axes = {"z": 0, "y": 1, "x": 2}
    if not on_tiles(reductions):
        return pack_small(reductions, width)
    for each in reductions:
        block = (each.rows, each.cols)
        one, two, lead = axes[each.order[0]], axes[each.order[1]], each.lead

        def base_map(step, at, one=one, two=two, lead=lead):
            return (lead + at[one], at[two], step, 0, 0)

        def first_map(step, at, two=two):
            return (at[two], step, 0, 0)

        operands += each.base + each.first + each.second
        specs += [pl.BlockSpec((None, None, None, *block), base_map)] * len(each.base)
        specs += [pl.BlockSpec((None, None, *block), first_map)] * len(each.first)
        specs += [pl.BlockSpec((None, *block), lambda step, at: (step, 0, 0))] * len(each.second)
        counts.append(len(each.base) + len(each.first) + len(each.second))
    rows = sum(packed_rows(each) * (each.cols // width) for each in reductions)
    place_array = jnp.stack([place["z"], place["y"], place["x"]]).astype(jnp.int32)
    return pl.pallas_call(
        functools.partial(pack_kernel, counts),
        grid_spec=pltpu.PrefetchScalarGridSpec(
            num_scalar_prefetch=1,
            grid=(line,),
            in_specs=specs,
            out_specs=pl.BlockSpec((None, rows, width), lambda step, at: (step, 0, 0)),
        ),
        out_shape=sds((line, rows, width), BF),
        compiler_params=params(),
        cost_estimate=cost(0, operands),
        name="pack_quarters",
    )(place_array, *operands)


def along_z(packed, sizes):
    return lax.all_to_all(packed, "dev", 0, 0, axis_index_groups=lines(sizes, "z"), tiled=True)


def line_sum(pieces):
    return total([pieces[number] for number in range(pieces.shape[0])])


def unpack(ref, at, rows, cols):
    width = ref.shape[1]
    parts = []
    for _ in range(0, cols, width):
        parts.append(ref[at : at + rows, :].astype(F32))
        at += -(-rows // 16) * 16
    return (parts[0] if len(parts) == 1 else jnp.concatenate(parts, axis=1)), at


def line_of(piece, sizes):
    return [piece] + [shifted(piece, sizes, "z", by) for by in range(1, sizes["z"])]


def plane_of(line, sizes):
    rows = line[0].shape[0] // 2
    found = []
    for half, (_, second) in enumerate(ORDERS):
        own = jnp.stack([each[half * rows : (half + 1) * rows] for each in line])
        found.append([own] + [shifted(own, sizes, second, by) for by in range(1, sizes[second])])
    return found


def all_of(planes, sizes):
    found = []
    for plane, (first, _) in zip(planes, ORDERS):
        arrays = list(plane)
        for by in range(1, sizes[first]):
            arrays += [shifted(array, sizes, first, by) for array in plane]
        found.append(arrays)
    return found


def put_part(outs, kind, flat, half, source, at):
    if kind in ("up", "down"):
        outs[kind][flat], at = unpack(source, at, *outs[kind].shape[1:])
        return at
    values, at = unpack(source, at, *outs["in"].shape[1:])
    if kind == "low":
        outs["in"][flat] = values
    else:

        @pl.when(flat < half)
        def _():
            outs["in"][2 * half + flat] = values

        @pl.when(flat >= half)
        def _():
            outs["out"][flat - half] = values

    return at


def assemble_kernel(sizes, names, kinds, place_ref, *refs):
    outs = dict(zip(names, refs[len(refs) - len(names) :]))
    axes = {"z": 0, "y": 1, "x": 2}
    start = 0
    for (one, two), wanted in zip(ORDERS, kinds):
        size_a, size_b = sizes[one], sizes[two]
        half = size_a * size_b // 2
        for by_a in range(size_a):
            for by_b in range(size_b):
                source = refs[start]
                start += 1
                at_a = lax.rem(place_ref[axes[one]] + (size_a - by_a), size_a)
                at_b = lax.rem(place_ref[axes[two]] + (size_b - by_b), size_b)
                at = 0
                for kind in wanted:
                    at = put_part(outs, kind, at_a * size_b + at_b, half, source, at)


def assemble(found, kinds, layers, shapes, sizes, place, earlier):
    names = list(layers)
    plane = sizes["x"] * sizes["y"]
    line = sizes["z"]
    counts = {"up": plane, "down": plane, "in": 3 * plane // 2, "out": plane // 2}
    place_array = jnp.stack([place["z"], place["y"], place["x"]]).astype(jnp.int32)
    kept = [name for name in names if name in earlier]
    pieces = found[0] + found[1]

    def owner(step, at):
        return lax.rem(at[0] + (line - step), line)

    def at_layer(layer):
        return lambda step, at: (layer, 0, owner(step, at), 0, 0)

    done = pl.pallas_call(
        functools.partial(assemble_kernel, sizes, names, kinds),
        grid_spec=pltpu.PrefetchScalarGridSpec(
            num_scalar_prefetch=1,
            grid=(line,),
            in_specs=[pl.BlockSpec((None, *pieces[0].shape[1:]), lambda step, at: (step, 0, 0))] * len(pieces)
            + [pl.BlockSpec(memory_space=pl.ANY)] * len(kept),
            out_specs=[
                pl.BlockSpec((None, counts[name], None, *shapes[name]), at_layer(layers[name])) for name in names
            ],
        ),
        out_shape=[sds((2, counts[name], line, *shapes[name]), F32) for name in names],
        input_output_aliases={1 + len(pieces) + number: names.index(name) for number, name in enumerate(kept)},
        compiler_params=params(),
        cost_estimate=cost(0, pieces * 3),
        name="assemble_" + "_".join(names),
    )(place_array, *pieces, *[earlier[name] for name in kept])
    return {**earlier, **dict(zip(names, done))}


def layer_forward(layer, x, ends, own, other, small, gain, shift):
    query, key, value, probs, mixed, normed1, rate1 = attend_forward(layer, x, ends, own, other, small, shift)
    act, dg, result, normed2, rate2 = feed_forward(layer, normed1, own, other, small, gain, shift)
    return result, (query, key, value, probs, mixed), (normed2, rate2, normed1, rate1, act, dg)


def prepare_small(b_in, b_up, rel_table):
    layers, _, local = b_in.shape
    units = b_up.shape[1]
    heads, span = rel_table.shape[1:]
    steps = local // LANES
    tile = units // steps
    head_dim = local // heads
    flat = jnp.concatenate([b_in.astype(F32).reshape(-1), b_up.astype(F32).reshape(-1), rel_table.reshape(-1)])
    again = swap(flat)

    def parts(vector):
        cut = layers * 2 * local
        end = cut + layers * units
        return (
            vector[:cut].reshape(layers, 2, steps, LANES).transpose(0, 2, 1, 3),
            vector[cut:end].reshape(layers, units // tile, 1, tile),
            vector[end:].reshape(layers, steps, heads // steps, span),
        )

    own, other = parts(flat), parts(again)
    tables = jnp.concatenate([own[2], other[2]], axis=2)
    return {
        "head_dim": head_dim,
        "b_in": jnp.concatenate([own[0], other[0]], axis=3),
        "b_up": jnp.concatenate([own[1], other[1]], axis=3),
        "table": [jnp.pad(tables[0], ((0, 0), (0, 0), (span // 2, span // 2)), mode="edge"), tables[1]],
    }


def small_pack_kernel(head_ref, *refs):
    inputs, outs = refs[:-2], refs[-2:]
    head = head_ref[0]
    row = 0
    for layer in (0, 1):
        gb, gbu, table, norms = inputs[4 * layer : 4 * layer + 4]
        steps, span, local = gb.shape[0], outs_span(table, layer), norms.shape[1] // 2
        tile, heads = gbu.shape[2] // 2, table.shape[1] // 2
        extra = (table.shape[2] - span) // 2
        for slot in range(2):
            for step in range(steps):
                for side, out in enumerate(outs):
                    out[row : row + 1, :] = gb[step, slot : slot + 1, side * LANES : (side + 1) * LANES]
                row += 1
        for step in range(gbu.shape[0]):
            for at in range(0, tile, LANES):
                for side, out in enumerate(outs):
                    out[row : row + 1, :] = gbu[step, :, side * tile + at : side * tile + at + LANES]
                row += 1
        lane = lax.broadcasted_iota(jnp.int32, (1, LANES), 1)
        for step in range(steps):
            for number in range(heads):
                for side, out in enumerate(outs):
                    values = table[step, side * heads + number : side * heads + number + 1, :]
                    for at in range(0, span, LANES):
                        part = values[:, extra + at : extra + at + LANES]
                        if extra and at == 0:
                            part = part + jnp.where(lane == 0, jnp.sum(values[:, :extra], axis=1, keepdims=True), 0.0)
                        if extra and at == span - LANES:
                            rest = jnp.sum(values[:, extra + span :], axis=1, keepdims=True)
                            part = part + jnp.where(lane == LANES - 1, rest, 0.0)
                        out[row + at // LANES : row + at // LANES + 1, :] = part
                row += span // LANES
        for number in range(6):
            for at in range(0, local, LANES):
                low = norms[number : number + 1, at : at + LANES]
                high = norms[number : number + 1, local + at : local + at + LANES]
                outs[0][row : row + 1, :] = jnp.where(head == 0, low, high)
                outs[1][row : row + 1, :] = jnp.where(head == 0, high, low)
                row += 1


def outs_span(table, layer):
    return table.shape[2] // 2 if layer == 0 else table.shape[2]


def small_pack(layers, head):
    flat = [array for grads in layers for array in grads]
    gb, gbu, table, norms = layers[1]
    half = gb.size // 2 + gbu.size // 2 + table.size // 2 + 6 * norms.shape[1] // 2
    shape = sds((2 * half // LANES, LANES), F32)
    return pl.pallas_call(
        small_pack_kernel,
        in_specs=[pl.BlockSpec(memory_space=pltpu.SMEM)] + [pl.BlockSpec(memory_space=pltpu.VMEM)] * len(flat),
        out_specs=[pl.BlockSpec(memory_space=pltpu.VMEM)] * 2,
        out_shape=[shape, shape],
        cost_estimate=cost(0, flat * 2),
        name="small_pack",
    )(head.astype(jnp.int32).reshape(1), *flat)


def small_unpack_kernel(total_ref, b_in, b_up, rel, gain, shift):
    row = 0
    for layer in (0, 1):
        for rows, out in ((b_in.shape[1], b_in), (1, b_up), (rel.shape[1], rel), (2, gain), (4, shift)):
            for number in range(rows):
                for at in range(0, out.shape[2], LANES):
                    out[layer, number : number + 1, at : at + LANES] = total_ref[row : row + 1, :]
                    row += 1


def small_unpack(total, b_in, b_up, rel, width):
    shapes = [b_in, (b_up[0], 1, b_up[1]), rel, (2, 2, width), (2, 4, width)]
    out = pl.pallas_call(
        small_unpack_kernel,
        out_shape=[sds(shape, F32) for shape in shapes],
        cost_estimate=cost(0, [total, total]),
        name="small_unpack",
    )(total)
    return out[0], out[1].reshape(b_up), out[2], out[3], out[4]


def per_device(
    tokens, lengths, w_in, b_in, w_out, w_up, b_up, w_down, norm_gain, norm_bias, rel_table, d_pooled, d_skip
):
    devices = lax.axis_size("dev") * lax.axis_size("head")
    count, piece, width = tokens.shape
    pooled_piece = piece // 2
    rows = -(-count // devices)
    padded = rows * devices
    extra = padded - count
    span = rel_table.shape[2]
    head = lax.axis_index("head")
    index = head * lax.axis_size("dev") + lax.axis_index("dev")
    both = ("head", "dev")
    norm_cols = width // lax.axis_size("head")

    def with_extra(array):
        return jnp.pad(array, ((0, extra), (0, 0), (0, 0)))

    def to_rows(array):
        return lax.all_to_all(array, both, split_axis=0, concat_axis=1, tiled=True)

    def to_places(array):
        return lax.all_to_all(array, both, split_axis=1, concat_axis=0, tiled=True)[:count]

    sizes = grid_sizes(lax.axis_size("dev"))
    place = place_of(lax.axis_index("dev"), sizes)
    x0 = to_rows(with_extra(tokens))
    own = {"w_in": w_in, "w_out": w_out, "w_up": w_up, "w_down": w_down}
    other = {name: swap(array) for name, array in own.items()}
    small = prepare_small(b_in, b_up, rel_table)
    second_grad = plain_call(
        pair_sum_kernel,
        sds((count * pooled_piece, width), BF),
        d_skip.reshape(count * piece, width),
        d_pooled.reshape(count * pooled_piece, width),
    ).reshape(count, pooled_piece, width)
    x0, second_grad = lax.optimization_barrier((x0, with_extra(second_grad)))
    grad_rows = to_rows(second_grad)
    ends = lax.dynamic_slice_in_dim(jnp.pad(jnp.cumsum(lengths, axis=1), ((0, extra), (0, 0))), index * rows, rows, 0)

    first, keep_a0, keep_f0 = layer_forward(0, x0, ends, own, other, small, norm_gain[0], norm_bias[0])
    pooled = span // 2
    x1 = first.reshape(rows, pooled, width)
    second, keep_a1, keep_f1 = layer_forward(1, x1, ends, own, other, small, norm_gain[1], norm_bias[1])
    pooled_out = to_places(second.reshape(rows, pooled, width))

    def feed_reductions(up, down):
        return [Reduction(up, sizes, place, ORDERS[0]), Reduction(down, sizes, place, ORDERS[1])]

    def attend_reductions(array):
        return [Reduction(array, sizes, place, order, half, 2) for half, order in enumerate(ORDERS)]

    def moves(group, level, sends):
        return [each.moves(level, arrays) for each, arrays in zip(group, sends)]

    def first_sends(group, arrays):
        for each, array in zip(group, arrays):
            each.absorb(array)
        return [each.first_sends() for each in group]

    def second_sends(group, received):
        for each, arrays in zip(group, received):
            each.first = arrays
        return [each.second_sends() for each in group]

    def settle_second(group, received):
        for each, arrays in zip(group, received):
            each.second = arrays

    grad = grad_rows.reshape(rows * pooled, width)
    outs = feed_backward(1, grad, keep_f1, own, other, small, norm_gain[1], norm_bias[1])
    outs, pooled_out = tie(outs, pooled_out)
    gwu_a, gwu_b, gwd_a, gwd_b, gbu1, grad_att, grad_resid, norms1 = outs
    feed1 = feed_reductions(gwu_a, gwd_a)
    sends_f1 = first_sends(feed1, [swap(gwu_b), swap(gwd_b)])
    outs = attend_backward(
        1, grad_att, grad_resid, x1, keep_a1, own, other, small, after=jax.tree.leaves(sends_f1)
    )
    outs, got_f1 = tie(outs, moves(feed1, 0, sends_f1))
    g_a, g_b, gb1, table1, grad = outs
    att1 = attend_reductions(g_a)
    g_b = swap(g_b)
    sends_f1, sends_a1 = second_sends(feed1, got_f1), first_sends(att1, [g_b, g_b])
    outs = feed_backward(
        0, grad, keep_f0, own, other, small, norm_gain[0], norm_bias[0], after=jax.tree.leaves((sends_a1, sends_f1))
    )
    outs, got_a1, got_f1 = tie(outs, moves(att1, 0, sends_a1), moves(feed1, 1, sends_f1))
    gwu_a, gwu_b, gwd_a, gwd_b, gbu0, grad_att, grad_resid, norms0 = outs
    feed0 = feed_reductions(gwu_a, gwd_a)
    settle_second(feed1, got_f1)
    packed1, sends_a1 = pack(feed1, place), second_sends(att1, got_a1)
    sends_f0 = first_sends(feed0, [swap(gwu_b), swap(gwd_b)])
    outs = attend_backward(
        0, grad_att, grad_resid, x0, keep_a0, own, other, small,
        after=jax.tree.leaves((sends_f0, sends_a1, packed1)),
        places=devices if piece % 16 == 0 else 0,
    )
    outs, got_f0, got_a1, pieces1 = tie(
        outs, moves(feed0, 0, sends_f0), moves(att1, 1, sends_a1), along_z(packed1, sizes)
    )
    g_a, g_b, gb0, table0, grad = outs
    att0 = attend_reductions(g_a)
    settle_second(att1, got_a1)
    line1 = line_of(line_sum(pieces1), sizes)
    g_b = swap(g_b)
    sends_f0, sends_a0 = second_sends(feed0, got_f0), first_sends(att0, [g_b, g_b])
    got_a0, got_f0, line1 = tie(moves(att0, 0, sends_a0), moves(feed0, 1, sends_f0), line1)
    settle_second(feed0, got_f0)
    mine, theirs = small_pack(((gb0, gbu0, table0, norms0), (gb1, gbu1, table1, norms1)), head)
    packed10 = pack([att1[0], feed0[0], att1[1], feed0[1]], place)
    sends_a0 = second_sends(att0, got_a0)
    pieces10, got_a0, plane1, theirs = tie(
        along_z(packed10, sizes), moves(att0, 1, sends_a0), plane_of(line1, sizes), swap(theirs)
    )
    settle_second(att0, got_a0)
    line10, pieces0, found1, grad, total_small = tie(
        line_of(line_sum(pieces10), sizes),
        along_z(pack(att0, place), sizes),
        all_of(plane1, sizes),
        grad,
        pair_sum(mine + theirs, sizes, "x", 1),
    )
    total_small = pair_sum_rest(total_small, sizes, "x")
    plane10, line0, total_small, grad = tie(
        plane_of(line10, sizes), line_of(line_sum(pieces0), sizes), pair_sum(total_small, sizes, "y", 1), grad
    )
    total_small = pair_sum_rest(total_small, sizes, "y")
    whole_tiles = on_tiles(feed1 + att1)
    block = {
        "up": (feed1[0].rows, feed1[0].cols),
        "down": (feed1[1].rows, feed1[1].cols),
        "in": (att1[0].rows, att1[0].cols),
        "out": (att1[0].rows, att1[0].cols),
    }
    found10, plane0, grad, total_small = tie(all_of(plane10, sizes), plane_of(line0, sizes), grad, total_small)
    if piece % 16 == 0:
        grad_in = lax.all_to_all(grad, both, split_axis=0, concat_axis=0, tiled=True)
        grad_in = grad_in.reshape(padded, piece, width)[:count]
    else:
        grad_in = to_places(grad.reshape(rows, span, width))
    sums = {}
    if whole_tiles:
        sums = assemble(found1, (("up",), ("down",)), {"up": 1, "down": 1}, block, sizes, place, sums)
    if whole_tiles:
        layers = {"up": 0, "down": 0, "in": 1, "out": 1}
        sums = assemble(found10, (("low", "up"), ("high", "down")), layers, block, sizes, place, sums)
    found0, total_small, sums = tie(all_of(plane0, sizes), pair_sum(total_small, sizes, "z", 1), sums)
    total_small = pair_sum_rest(total_small, sizes, "z")
    flat_tokens = tokens.reshape(count * piece, width)
    skips = plain_call(
        skip_kernel,
        (sds(flat_tokens.shape, BF), sds(flat_tokens.shape, BF)),
        flat_tokens,
        d_skip.reshape(count * piece, width),
        pooled_out.reshape(count * pooled_piece, width),
        grad_in.reshape(count * piece, width),
    )
    skip_sum, d_input = skips
    g_b_in, g_b_up, g_rel, g_gain, g_bias = small_unpack(
        total_small, b_in.shape, b_up.shape, rel_table.shape, norm_cols
    )

    if whole_tiles:
        sums = assemble(found0, (("low",), ("high",)), {"in": 0, "out": 0}, block, sizes, place, sums)
        g_w_up, g_w_down, g_w_in, g_w_out = [sums[name] for name in ("up", "down", "in", "out")]
    else:
        gathered = [lax.all_gather(line[0], "dev", axis=0, tiled=False) for line in (line1, line10, line0)]
        g_w_up, g_w_down, g_w_in, g_w_out = assemble_small(
            *gathered, feed1, att1, feed0, att0, sizes
        )

    return (
        pooled_out,
        skip_sum.reshape(tokens.shape),
        d_input.reshape(tokens.shape),
        g_w_in.reshape(w_in.shape),
        g_b_in,
        g_w_out.reshape(2, width, w_in.shape[3]).transpose(0, 2, 1),
        g_w_up.reshape(w_up.shape),
        g_b_up,
        g_w_down.reshape(w_down.shape),
        g_gain,
        g_bias,
        g_rel,
    )


def solution(mesh):
    in_specs = (
        P(None, ("head", "dev"), None),
        P(),
        P(None, None, None, "head"),
        P(None, None, "head"),
        P(None, "head", None),
        P(None, None, "head"),
        P(None, "head"),
        P(None, "head", None),
        P(),
        P(),
        P(None, "head", None),
        P(None, ("head", "dev"), None),
        P(None, ("head", "dev"), None),
    )
    out_specs = (
        P(None, ("head", "dev"), None),
        P(None, ("head", "dev"), None),
        P(None, ("head", "dev"), None),
        P(None, None, None, "head"),
        P(None, None, "head"),
        P(None, "head", None),
        P(None, None, "head"),
        P(None, "head"),
        P(None, "head", None),
        P(None, None, "head"),
        P(None, None, "head"),
        P(None, "head", None),
    )
    return jax.shard_map(per_device, mesh=mesh, in_specs=in_specs, out_specs=out_specs, check_vma=False)
```
